256 devices in a mesh: seq: 64 (over y, z, core), head: 4 (over x).
Axes of the slice: x: 4, y: 4, z: 8, core: 2. Of those that a mesh axis runs over, the one named last changes fastest.
Arguments:
- queries: bfloat16 [8192, 64, 128], P('seq', 'head'), may hold values from -6 to 6
- keys: bfloat16 [8192, 64, 128], P('seq', 'head'), may hold values from -6 to 6
- values: bfloat16 [8192, 64, 128], P('seq', 'head'), may hold values from -15 to 15
- out_grad: bfloat16 [8192, 64, 128], P('seq', 'head'), may hold values from -6 to 6
Outputs:
- normed: bfloat16 [8192, 64, 128], P('seq', 'head')
- query_grad: bfloat16 [8192, 64, 128], P('seq', 'head')
- key_grad: bfloat16 [8192, 64, 128], P('seq', 'head')
- value_grad: bfloat16 [8192, 64, 128], P('seq', 'head')
The draws below stay inside these ranges and needn't reach their ends.
All inputs are finite; a program needn't handle non-finite values.
Results may differ from the reference program's by a relative error of at most 0.0058.
Values sent between devices are 32-bit elements; how exact they have to be, the bound alone decides.
A program may use at most 256 MiB of HBM per device.

```python
import math
import jax
import jax.numpy as jnp
from jax import lax

HEADS = 64
DH = 128
TOK_DEV = 128
TOKENS = 8192


def draw_values(key, part):
    key = jax.random.fold_in(key, 7)
    key_scale, key_base = jax.random.split(key, 2)
    col_scale = jnp.exp(jax.random.uniform(key_scale, (HEADS, DH), jnp.float32, math.log(0.3), math.log(3.0)))
    base = jnp.clip(jax.random.normal(key_base, (TOKENS, HEADS, DH), jnp.float32), -5.0, 5.0)
    drawn = base * col_scale
    return drawn.astype(jnp.bfloat16)


def levels(rng, shape, cuts, least, top_value):
    def one(axis_at, blocks):
        steps = jax.random.uniform(jax.random.fold_in(jax.random.fold_in(rng, 6), axis_at), (blocks,), jnp.float32, least / len(cuts), top_value / len(cuts))
        return jnp.repeat(jnp.exp(steps), shape[axis_at] // blocks).reshape((-1,) + (1,) * (len(shape) - axis_at - 1))

    level = one(*cuts[0])
    for cut in cuts[1:]:
        level = level * one(*cut)
    return level


def normal_values(key, shape, spread, reach, cuts=(), held_as=jnp.bfloat16):
    values = spread * jax.random.normal(key, shape, jnp.float32)
    if cuts:
        values = values * levels(key, shape, cuts, -0.22, 0.18)
    return jnp.clip(values, -reach, reach).astype(held_as)


def setup_inputs(seed: int = 0) -> dict:
    seeds = jax.random.split(jax.random.key(seed), 5)
    return {
        "queries": normal_values(seeds[0], (TOKENS, HEADS, DH), 1.0, 6.0, ((0, 64), (1, 4))),
        "keys": normal_values(seeds[1], (TOKENS, HEADS, DH), 1.0, 6.0, ((0, 64), (1, 4))),
        "values": draw_values(jax.random.fold_in(seeds[4], 71), 0),
        "out_grad": normal_values(seeds[3], (TOKENS, HEADS, DH), 1.0, 6.0, ((0, 64), (1, 4))),
    }


EPS = 1e-06

def reference(queries, keys, values, out_grad):
    blocks = TOKENS // TOK_DEV
    row_width = HEADS * DH
    causal = jnp.tril(jnp.ones((TOK_DEV, TOK_DEV), dtype=bool))
    query_blk = queries.reshape(blocks, TOK_DEV, HEADS, DH)
    key_blk = keys.reshape(blocks, TOK_DEV, HEADS, DH)
    value_blk = values.reshape(blocks, TOK_DEV, HEADS, DH)
    grad_blk = out_grad.reshape(blocks, TOK_DEV, HEADS, DH)

    def forward_step(carried, block_in):
        query_f, key_f, value_f, grad_f = [a.astype(jnp.float32) for a in block_in]
        scores = jnp.einsum('thd,shd->hts', query_f, key_f)
        weights = jnp.where(causal, scores, 0.0).astype(jnp.bfloat16)
        prior = carried.astype(jnp.bfloat16)
        attended = jnp.einsum('hts,she->the', weights.astype(jnp.float32), value_f)
        attended = attended + jnp.einsum('thd,hde->the', query_f, prior.astype(jnp.float32))
        square_sum = lax.optimization_barrier(jnp.sum(attended * attended, axis=(1, 2)))
        dot_sum = lax.optimization_barrier(jnp.sum(grad_f * attended, axis=(1, 2)))
        inv_rms = 1.0 / jnp.sqrt(square_sum / row_width + EPS)
        normed = (attended * inv_rms[:, None, None]).astype(jnp.bfloat16)
        factor = inv_rms * inv_rms * inv_rms * dot_sum / row_width
        att_grad = (inv_rms[:, None, None] * grad_f - attended * factor[:, None, None]).astype(jnp.bfloat16)
        own_state = jnp.einsum('thd,the->hde', key_f, value_f)
        return (carried + own_state, (normed, att_grad, prior))
    start = jnp.zeros((HEADS, DH, DH), jnp.float32)
    _, (normed, att_grads, priors) = lax.scan(forward_step, start, (query_blk, key_blk, value_blk, grad_blk))

    def backward_step(carried, block_in):
        query_b, key_b, value_b, att_b, prior = block_in
        query_f = query_b.astype(jnp.float32)
        key_f = key_b.astype(jnp.float32)
        value_f = value_b.astype(jnp.float32)
        att_f = att_b.astype(jnp.float32)
        prior_f = prior.astype(jnp.float32)
        later = carried.astype(jnp.bfloat16).astype(jnp.float32)
        scores = jnp.einsum('thd,shd->hts', query_f, key_f)
        weights = jnp.where(causal, scores, 0.0).astype(jnp.bfloat16).astype(jnp.float32)
        grad_scores = jnp.einsum('the,she->hts', att_f, value_f)
        masked = jnp.where(causal, grad_scores, 0.0).astype(jnp.bfloat16).astype(jnp.float32)
        query_grad = jnp.einsum('hts,shd->thd', masked, key_f) + jnp.einsum('the,hde->thd', att_f, prior_f)
        key_grad = jnp.einsum('hts,thd->shd', masked, query_f) + jnp.einsum('she,hde->shd', value_f, later)
        value_grad = jnp.einsum('hts,the->she', weights, att_f) + jnp.einsum('shd,hde->she', key_f, later)
        own_grad = jnp.einsum('thd,the->hde', query_f, att_f)
        outs = (query_grad.astype(jnp.bfloat16), key_grad.astype(jnp.bfloat16), value_grad.astype(jnp.bfloat16))
        return (carried + own_grad, outs)
    _, (query_grad, key_grad, value_grad) = lax.scan(backward_step, start, (query_blk, key_blk, value_blk, att_grads, priors), reverse=True)
    full = (TOKENS, HEADS, DH)
    return (normed.reshape(full), query_grad.reshape(full), key_grad.reshape(full), value_grad.reshape(full))
```

```python
import jax
import jax.numpy as jnp
from jax import lax
from jax.experimental import pallas as pl
from jax.experimental.pallas import tpu as pltpu
from jax.sharding import PartitionSpec as P

EPS = 1e-06
CHIPS = 32
TOK = 128
NH = 16
DH = 128
HALF = NH // 2
ROWS = HALF * DH // CHIPS
SPLIT = DH // ROWS
ROW_WIDTH = 64 * DH
MESH = pl.DeviceIdType.MESH
F32 = jnp.float32
BF16 = jnp.bfloat16


def mm(left, right, lc, rc):
    return lax.dot_general(
        left, right, (((lc,), (rc,)), ((), ())), preferred_element_type=F32
    )


def kernel(
    q_hbm, k_hbm, v_hbm, g_hbm,
    n_out, qg_out, kg_out, vg_out,
    q_in, k_in, v_in, g_in, n_vm, qg_vm, kg_vm, vg_vm,
    flat_a, flat_b, qh, kh, vh, gh, wts, att, agr, prior, kg_acc, vg_acc,
    state, sib, chip, owned, bases, base, share, other,
    acc, msg, sums,
    load_sem, store_sem, d2d_send, d2d_recv, a2a_send, a2a_recv, x_send, x_recv,
):
    seq, head = lax.axis_index("seq"), lax.axis_index("head")
    s, c = seq // 2, lax.rem(seq, 2)
    oc = 1 - c

    bar = pltpu.get_barrier_semaphore()

    def greet(i, _):
        t = lax.rem(s + i, CHIPS)
        pl.semaphore_signal(bar, inc=1, device_id=(2 * t + c, head), device_id_type=MESH)
        return 0

    pl.semaphore_signal(bar, inc=1, device_id=(2 * s + oc, head), device_id_type=MESH)
    for i in range(1, 4):
        pl.semaphore_signal(
            bar, inc=1, device_id=(seq, lax.rem(head + i, 4)), device_id_type=MESH
        )
    lax.fori_loop(1, CHIPS, greet, 0)

    loads = [
        pltpu.make_async_copy(src, dst, load_sem.at[i])
        for i, (src, dst) in enumerate(
            ((k_hbm, k_in), (v_hbm, v_in), (q_hbm, q_in), (g_hbm, g_in))
        )
    ]
    for ld in loads:
        ld.start()

    def flatten(src, flat):
        flat[...] = src[...].astype(F32).reshape(TOK * NH, DH)

    def pick(flat, h):
        return flat[pl.ds(h, TOK, stride=NH), :].astype(BF16)

    def over(count, body):
        def step(i, _):
            for u in range(4):
                body(4 * i + u)
            return 0

        lax.fori_loop(0, count // 4, step, 0)

    rows = lax.broadcasted_iota(jnp.int32, (TOK, TOK), 0)
    cols = lax.broadcasted_iota(jnp.int32, (TOK, TOK), 1)
    causal = cols <= rows

    def d2d(k, src, dst):
        return pltpu.make_async_remote_copy(
            src_ref=src, dst_ref=dst, send_sem=d2d_send.at[k], recv_sem=d2d_recv.at[k],
            device_id=(2 * s + oc, head), device_id_type=MESH,
        )

    def spread(k, src, dst):
        def send(i, _):
            t = lax.rem(s + i, CHIPS)
            pltpu.make_async_remote_copy(
                src_ref=src.at[t], dst_ref=dst.at[s], send_sem=a2a_send.at[k],
                recv_sem=a2a_recv.at[k], device_id=(2 * t + c, head), device_id_type=MESH,
            ).start()
            return 0

        lax.fori_loop(1, CHIPS, send, 0)
        dst[s] = src[s]

    def spread_wait(k, src, dst):
        return pltpu.make_async_remote_copy(
            src_ref=src.at[pl.ds(0, CHIPS - 1)], dst_ref=dst.at[pl.ds(0, CHIPS - 1)],
            send_sem=a2a_send.at[k], recv_sem=a2a_recv.at[k],
            device_id=(2 * s + oc, head), device_id_type=MESH,
        )

    def put_state(j, h, value):
        state[j, pl.ds(h * SPLIT, SPLIT)] = value.reshape(SPLIT, ROWS, DH)

    def scan(j, make_other, make_own, during_up, during_down, reverse):
        make_other()
        if j == 0:
            pl.semaphore_wait(bar, CHIPS - 1 + 4)
        out = d2d(2 * j, state.at[j, pl.ds(oc * CHIPS, CHIPS)], sib.at[j])
        out.start()
        make_own()
        out.wait_recv()
        chip[j] = state[j, pl.ds(c * CHIPS, CHIPS)] + sib[j]
        spread(2 * j, chip.at[j], owned.at[j])
        during_up()
        spread_wait(2 * j, chip.at[j], owned.at[j]).wait_recv()
        run = jnp.zeros((ROWS, DH), F32)
        for t in range(CHIPS - 1, -1, -1) if reverse else range(CHIPS):
            bases[j, t] = run
            run = run + owned[j, t]
        spread(2 * j + 1, bases.at[j], base.at[j])
        during_down()
        spread_wait(2 * j + 1, bases.at[j], base.at[j]).wait_recv()
        first = oc if reverse else c
        share[j] = base[j] + jnp.where(first == 0, state[j, pl.ds(c * CHIPS, CHIPS)], 0.0)
        back = d2d(2 * j + 1, share.at[j], other.at[j])
        back.start()
        base[j] = base[j] + jnp.where(first == 1, sib[j], 0.0)
        return out, back

    def scan_end(j, out, back):
        out.wait_send()
        back.wait_send()
        spread_wait(2 * j, chip.at[j], owned.at[j]).wait_send()
        spread_wait(2 * j + 1, bases.at[j], base.at[j]).wait_send()

    def head_of(ref, j, i):
        return ref[j, pl.ds(i * SPLIT, SPLIT)].reshape(DH, DH).astype(BF16)

    loads[0].wait()
    flatten(k_in, flat_a)
    loads[1].wait()
    flatten(v_in, flat_b)

    def make_state(h):
        kk, vv = pick(flat_a, h), pick(flat_b, h)
        kh[h], vh[h] = kk, vv
        put_state(0, h, mm(kk, vv, 0, 0))

    def local_attention():
        loads[2].wait()
        flatten(q_in, flat_a)

        def body(h):
            qq = pick(flat_a, h)
            qh[h] = qq
            w = jnp.where(causal, mm(qq, kh[h], 1, 1), 0.0).astype(BF16)
            wts[h] = w
            att[h] = mm(w, vh[h], 1, 0)

        over(NH, body)

    def load_grads():
        loads[3].wait()
        flatten(g_in, flat_b)

        def body(h):
            gh[h] = pick(flat_b, h)

        over(NH, body)
        acc[...] = jnp.zeros_like(acc)

    out0, back0 = scan(
        0,
        lambda: over(HALF, lambda i: make_state(oc * HALF + i)),
        lambda: over(HALF, lambda i: make_state(c * HALF + i)),
        local_attention,
        load_grads,
        False,
    )

    def attend(h, pr):
        prior[h] = pr
        a = att[h] + mm(qh[h], pr, 1, 0)
        att[h] = a
        acc[0] += a * a
        acc[1] += a * gh[h].astype(F32)

    over(HALF, lambda i: attend(c * HALF + i, head_of(base, 0, i)))
    back0.wait_recv()
    over(HALF, lambda i: attend(oc * HALF + i, head_of(other, 0, i)))

    sq = jnp.sum(acc[0], axis=1, keepdims=True)
    dt = jnp.sum(acc[1], axis=1, keepdims=True)
    packed = jnp.where(cols == 0, sq, jnp.where(cols == 1, dt, 0.0))
    msg[...] = jnp.transpose(packed)[0:8]
    xs = [
        pltpu.make_async_remote_copy(
            src_ref=msg, dst_ref=sums.at[i], send_sem=x_send.at[i], recv_sem=x_recv.at[i],
            device_id=(seq, lax.rem(head + i + 1, 4)), device_id_type=MESH,
        )
        for i in range(3)
    ]
    for x in xs:
        x.start()
    for x in xs:
        x.wait_recv()
    total = msg[...] + sums[0] + sums[1] + sums[2]
    inv = 1.0 / jnp.sqrt(total[0:1] / ROW_WIDTH + EPS)
    fac = inv * inv * inv * total[1:2] / ROW_WIDTH
    both = jnp.transpose(jnp.where(rows == 0, inv, jnp.where(rows == 1, fac, 0.0)))
    inv_col, fac_col = both[:, 0:1], both[:, 1:2]

    def make_grad(h):
        ag = (inv_col * gh[h].astype(F32) - att[h] * fac_col).astype(BF16)
        agr[h] = ag
        put_state(1, h, mm(qh[h], ag, 0, 0))

    def query_side():
        def body(h):
            ag = agr[h]
            m = jnp.where(causal, mm(ag, vh[h], 1, 1), 0.0).astype(BF16)
            flat_a[pl.ds(h, TOK, stride=NH), :] = mm(m, kh[h], 1, 0) + mm(ag, prior[h], 1, 1)
            flat_b[pl.ds(h, TOK, stride=NH), :] = att[h] * inv_col
            kg_acc[h] = mm(m, qh[h], 0, 0)
            vg_acc[h] = mm(wts[h], ag, 0, 0)

        over(NH, body)

    stores = [
        pltpu.make_async_copy(src, dst, store_sem.at[i])
        for i, (src, dst) in enumerate(
            ((n_vm, n_out), (qg_vm, qg_out), (kg_vm, kg_out), (vg_vm, vg_out))
        )
    ]

    def emit(i, flat, ref):
        ref[...] = flat[...].reshape(TOK, NH, DH).astype(BF16)
        stores[i].start()

    def write_two():
        emit(0, flat_b, n_vm)
        emit(1, flat_a, qg_vm)

    out1, back1 = scan(
        1,
        lambda: over(HALF, lambda i: make_grad(oc * HALF + i)),
        lambda: over(HALF, lambda i: make_grad(c * HALF + i)),
        query_side,
        write_two,
        True,
    )

    def finish(h, lt):
        flat_a[pl.ds(h, TOK, stride=NH), :] = kg_acc[h] + mm(vh[h], lt, 1, 1)
        flat_b[pl.ds(h, TOK, stride=NH), :] = vg_acc[h] + mm(kh[h], lt, 1, 0)

    over(HALF, lambda i: finish(c * HALF + i, head_of(base, 1, i)))
    back1.wait_recv()
    over(HALF, lambda i: finish(oc * HALF + i, head_of(other, 1, i)))
    emit(2, flat_a, kg_vm)
    emit(3, flat_b, vg_vm)

    scan_end(0, out0, back0)
    scan_end(1, out1, back1)
    for x in xs:
        x.wait_send()
    for st in stores:
        st.wait()


def shards(queries, keys, values, out_grad):
    shape = (TOK, NH, DH)
    half = (CHIPS, ROWS, DH)
    vm = pltpu.VMEM
    dma = pltpu.SemaphoreType.DMA
    hm = (NH, TOK, DH)
    return pl.pallas_call(
        kernel,
        out_shape=[jax.ShapeDtypeStruct(shape, BF16)] * 4,
        in_specs=[pl.BlockSpec(memory_space=pl.ANY)] * 4,
        out_specs=[pl.BlockSpec(memory_space=pl.ANY)] * 4,
        scratch_shapes=[vm(shape, BF16)] * 8
        + [vm((TOK * NH, DH), F32)] * 2
        + [vm(hm, BF16)] * 5
        + [vm(hm, F32), vm(hm, BF16), vm(hm, BF16), vm(hm, F32), vm(hm, F32)]
        + [vm((2, 2 * CHIPS, ROWS, DH), F32)]
        + [vm((2,) + half, F32)] * 7
        + [vm((2, TOK, DH), F32), vm((8, TOK), F32), vm((3, 8, TOK), F32)]
        + [dma((4,)), dma((4,)), dma((4,)), dma((4,)), dma((4,)), dma((4,)), dma((3,)), dma((3,))],
        compiler_params=pltpu.CompilerParams(
            collective_id=0, has_side_effects=True, vmem_limit_bytes=48 << 20
        ),
    )(queries, keys, values, out_grad)


def solution(mesh):
    spec = P("seq", "head", None)
    return jax.shard_map(
        shards, mesh=mesh, in_specs=(spec,) * 4, out_specs=(spec,) * 4, check_vma=False
    )
```

```python
import jax
import jax.numpy as jnp
from jax import lax
from jax.experimental import pallas as pl
from jax.experimental.pallas import tpu as pltpu
from jax.sharding import PartitionSpec as P

EPS = 1e-06
DELIVER = 4
CHIPS = 32
TOK = 128
NH = 16
DH = 128
HALF = NH // 2
CHUNKS = 2
CH = HALF // CHUNKS
ROWS = CH * DH // CHIPS
SPLIT = DH // ROWS
ROW_WIDTH = 64 * DH
MESH = pl.DeviceIdType.MESH
F32 = jnp.float32
BF16 = jnp.bfloat16


def mm(left, right, lc, rc):
    return lax.dot_general(
        left, right, (((lc,), (rc,)), ((), ())), preferred_element_type=F32
    )


def kernel(
    q_hbm, k_hbm, v_hbm, g_hbm,
    n_out, qg_out, kg_out, vg_out,
    q_in, k_in, v_in, g_in, n_vm, qg_vm, kg_vm, vg_vm,
    flat_a, flat_b, qh, kh, vh, gh, wts, att, agr, prior, kg_acc, vg_acc,
    given, state, sib, chip, owned, bases, base, share, other,
    acc, msg, sums,
    load_sem, store_sem, d2d_send, d2d_recv, a2a_send, a2a_recv, x_send, x_recv,
):
    seq, head = lax.axis_index("seq"), lax.axis_index("head")
    s, c = seq // 2, lax.rem(seq, 2)
    oc = 1 - c

    bar = pltpu.get_barrier_semaphore()

    def greet(i, _):
        t = lax.rem(s + i, CHIPS)
        pl.semaphore_signal(bar, inc=1, device_id=(2 * t + c, head), device_id_type=MESH)
        return 0

    pl.semaphore_signal(bar, inc=1, device_id=(2 * s + oc, head), device_id_type=MESH)
    for i in range(1, 4):
        pl.semaphore_signal(
            bar, inc=1, device_id=(seq, lax.rem(head + i, 4)), device_id_type=MESH
        )
    lax.fori_loop(1, CHIPS, greet, 0)

    loads = [
        pltpu.make_async_copy(src, dst, load_sem.at[i])
        for i, (src, dst) in enumerate(
            ((k_hbm, k_in), (v_hbm, v_in), (q_hbm, q_in), (g_hbm, g_in))
        )
    ]
    for ld in loads:
        ld.start()

    def flatten(src, flat):
        flat[...] = src[...].astype(F32).reshape(TOK * NH, DH)

    def pick(flat, h):
        return flat[pl.ds(h, TOK, stride=NH), :].astype(BF16)

    def over(body):
        def step(i, _):
            for u in range(4):
                body(4 * i + u)
            return 0

        lax.fori_loop(0, NH // 4, step, 0)

    rows = lax.broadcasted_iota(jnp.int32, (TOK, TOK), 0)
    cols = lax.broadcasted_iota(jnp.int32, (TOK, TOK), 1)
    causal = cols <= rows

    def d2d(j, way, n, src, dst):
        return pltpu.make_async_remote_copy(
            src_ref=src.at[j, n], dst_ref=dst.at[j, n], send_sem=d2d_send.at[j, way, n],
            recv_sem=d2d_recv.at[j, way, n], device_id=(2 * s + oc, head), device_id_type=MESH,
        )

    def spread(j, way, n, src, dst):
        def send(i, _):
            t = lax.rem(s + i, CHIPS)
            pltpu.make_async_remote_copy(
                src_ref=src.at[j, n, t], dst_ref=dst.at[j, n, s],
                send_sem=a2a_send.at[j, way, n], recv_sem=a2a_recv.at[j, way, n],
                device_id=(2 * t + c, head), device_id_type=MESH,
            ).start()
            return 0

        lax.fori_loop(1, CHIPS, send, 0)
        dst[j, n, s] = src[j, n, s]

    def spread_all(j, way, n, src, dst):
        return pltpu.make_async_remote_copy(
            src_ref=src.at[j, n, pl.ds(0, CHIPS - 1)], dst_ref=dst.at[j, n, pl.ds(0, CHIPS - 1)],
            send_sem=a2a_send.at[j, way, n], recv_sem=a2a_recv.at[j, way, n],
            device_id=(2 * s + oc, head), device_id_type=MESH,
        )

    def put_state(ref, j, n, i, value):
        ref[j, n, pl.ds(i * SPLIT, SPLIT)] = value.reshape(SPLIT, ROWS, DH)

    def head_of(ref, j, n, i):
        return ref[j, n, pl.ds(i * SPLIT, SPLIT)].reshape(DH, DH).astype(BF16)

    def scan(j, make, during_up, during_down, use, reverse):
        for n in range(CHUNKS):
            for i in range(CH):
                put_state(given, j, n, i, make(oc * HALF + n * CH + i))
            if j == 0 and n == 0:
                pl.semaphore_wait(bar, CHIPS - 1 + 4)
            d2d(j, 0, n, given, sib).start()
            for i in range(CH):
                put_state(state, j, n, i, make(c * HALF + n * CH + i))
        for n in range(CHUNKS):
            d2d(j, 0, n, given, sib).wait_recv()
            chip[j, n] = state[j, n] + sib[j, n]
            spread(j, 0, n, chip, owned)
        during_up()
        for n in range(CHUNKS):
            spread_all(j, 0, n, chip, owned).wait_recv()
            run = jnp.zeros((ROWS, DH), F32)
            for t in range(CHIPS - 1, -1, -1) if reverse else range(CHIPS):
                bases[j, n, t] = run
                run = run + owned[j, n, t]
            spread(j, 1, n, bases, base)
        during_down()
        first = oc if reverse else c
        for n in range(CHUNKS):
            spread_all(j, 1, n, bases, base).wait_recv()
            share[j, n] = base[j, n] + jnp.where(first == 0, state[j, n], 0.0)
            d2d(j, 1, n, share, other).start()
            base[j, n] = base[j, n] + jnp.where(first == 1, sib[j, n], 0.0)
            for i in range(CH):
                use(c * HALF + n * CH + i, head_of(base, j, n, i))
        for n in range(CHUNKS):
            d2d(j, 1, n, share, other).wait_recv()
            for i in range(CH):
                use(oc * HALF + n * CH + i, head_of(other, j, n, i))

    def scan_end(j):
        for n in range(CHUNKS):
            d2d(j, 0, n, given, sib).wait_send()
            d2d(j, 1, n, share, other).wait_send()
            spread_all(j, 0, n, chip, owned).wait_send()
            spread_all(j, 1, n, bases, base).wait_send()

    loads[0].wait()
    flatten(k_in, flat_a)
    loads[1].wait()
    flatten(v_in, flat_b)

    def make_state(h):
        kk, vv = pick(flat_a, h), pick(flat_b, h)
        kh[h], vh[h] = kk, vv
        return mm(kk, vv, 0, 0)

    def local_attention():
        loads[2].wait()
        flatten(q_in, flat_a)

        def body(h):
            qq = pick(flat_a, h)
            qh[h] = qq
            w = jnp.where(causal, mm(qq, kh[h], 1, 1), 0.0).astype(BF16)
            wts[h] = w
            att[h] = mm(w, vh[h], 1, 0)

        over(body)

    def load_grads():
        loads[3].wait()
        flatten(g_in, flat_b)

        def body(h):
            gh[h] = pick(flat_b, h)

        over(body)
        acc[...] = jnp.zeros_like(acc)

    def attend(h, pr):
        prior[h] = pr
        a = att[h] + mm(qh[h], pr, 1, 0)
        att[h] = a
        acc[0] += a * a
        acc[1] += a * gh[h].astype(F32)

    scan(0, make_state, local_attention, load_grads, attend, False)

    sq = jnp.sum(acc[0], axis=1, keepdims=True)
    dt = jnp.sum(acc[1], axis=1, keepdims=True)
    packed = jnp.where(cols == 0, sq, jnp.where(cols == 1, dt, 0.0))
    msg[...] = jnp.transpose(packed)[0:8]
    xs = [
        pltpu.make_async_remote_copy(
            src_ref=msg, dst_ref=sums.at[i], send_sem=x_send.at[i], recv_sem=x_recv.at[i],
            device_id=(seq, lax.rem(head + i + 1, 4)), device_id_type=MESH,
        )
        for i in range(3)
    ]
    for x in xs:
        x.start()
    for x in xs:
        x.wait_recv()
    total = msg[...] + sums[0] + sums[1] + sums[2]
    inv = 1.0 / jnp.sqrt(total[0:1] / ROW_WIDTH + EPS)
    fac = inv * inv * inv * total[1:2] / ROW_WIDTH
    both = jnp.transpose(jnp.where(rows == 0, inv, jnp.where(rows == 1, fac, 0.0)))
    inv_col, fac_col = both[:, 0:1], both[:, 1:2]

    def make_grad(h):
        ag = (inv_col * gh[h].astype(F32) - att[h] * fac_col).astype(BF16)
        agr[h] = ag
        return mm(qh[h], ag, 0, 0)

    def query_side():
        def body(h):
            ag = agr[h]
            m = jnp.where(causal, mm(ag, vh[h], 1, 1), 0.0).astype(BF16)
            flat_a[pl.ds(h, TOK, stride=NH), :] = mm(m, kh[h], 1, 0) + mm(ag, prior[h], 1, 1)
            flat_b[pl.ds(h, TOK, stride=NH), :] = att[h] * inv_col
            kg_acc[h] = mm(m, qh[h], 0, 0)
            vg_acc[h] = mm(wts[h], ag, 0, 0)

        over(body)

    stores = [
        pltpu.make_async_copy(src, dst, store_sem.at[i])
        for i, (src, dst) in enumerate(
            ((n_vm, n_out), (qg_vm, qg_out), (kg_vm, kg_out), (vg_vm, vg_out))
        )
    ]

    def emit(i, flat, ref):
        ref[...] = flat[...].reshape(TOK, NH, DH).astype(BF16)
        stores[i].start()

    def write_two():
        emit(0, flat_b, n_vm)
        emit(1, flat_a, qg_vm)

    def finish(h, lt):
        flat_a[pl.ds(h, TOK, stride=NH), :] = kg_acc[h] + mm(vh[h], lt, 1, 1)
        flat_b[pl.ds(h, TOK, stride=NH), :] = vg_acc[h] + mm(kh[h], lt, 1, 0)

    scan(1, make_grad, query_side, write_two, finish, True)
    emit(2, flat_a, kg_vm)
    emit(3, flat_b, vg_vm)

    scan_end(0)
    scan_end(1)
    for x in xs:
        x.wait_send()
    for st in stores:
        st.wait()


def deliver(*refs):
    sem = refs[8]
    copies = [pltpu.make_async_copy(refs[i], refs[4 + i], sem.at[i]) for i in range(4)]
    for cp in copies:
        cp.start()
    for cp in copies:
        cp.wait()


def shards(queries, keys, values, out_grad):
    shape = (TOK, NH, DH)
    half = (2, CHUNKS, CHIPS, ROWS, DH)
    per = (2, 2, CHUNKS)
    vm = pltpu.VMEM
    dma = pltpu.SemaphoreType.DMA
    hm = (NH, TOK, DH)
    results = pl.pallas_call(
        kernel,
        out_shape=[jax.ShapeDtypeStruct(shape, BF16)] * 4,
        in_specs=[pl.BlockSpec(memory_space=pltpu.HBM)] * 4,
        out_specs=[pl.BlockSpec(memory_space=pl.ANY)] * 4,
        scratch_shapes=[vm(shape, BF16)] * 8
        + [vm((TOK * NH, DH), F32)] * 2
        + [vm(hm, BF16)] * 5
        + [vm(hm, F32), vm(hm, BF16), vm(hm, BF16), vm(hm, F32), vm(hm, F32)]
        + [vm(half, F32)] * 9
        + [vm((2, TOK, DH), F32), vm((8, TOK), F32), vm((3, 8, TOK), F32)]
        + [dma((4,)), dma((4,)), dma(per), dma(per), dma(per), dma(per), dma((3,)), dma((3,))],
        compiler_params=pltpu.CompilerParams(
            collective_id=0, has_side_effects=True, vmem_limit_bytes=48 << 20
        ),
    )(*[pltpu.with_memory_space_constraint(x, pltpu.HBM) for x in (queries, keys, values, out_grad)])
    block = pl.BlockSpec((TOK // DELIVER, NH, DH), lambda i: (i, 0, 0))
    return pl.pallas_call(
        deliver,
        out_shape=[jax.ShapeDtypeStruct(shape, BF16)] * 4,
        in_specs=[pl.BlockSpec(memory_space=pltpu.VMEM)] * 4,
        out_specs=[pl.BlockSpec(memory_space=pl.ANY)] * 4,
        scratch_shapes=[dma((4,))],
        compiler_params=pltpu.CompilerParams(vmem_limit_bytes=8 << 20),
    )(*results)


def solution(mesh):
    spec = P("seq", "head", None)
    return jax.shard_map(
        shards, mesh=mesh, in_specs=(spec,) * 4, out_specs=(spec,) * 4, check_vma=False
    )
```

```python
import jax
import jax.numpy as jnp
from jax import lax
from jax.experimental import pallas as pl
from jax.experimental.pallas import tpu as pltpu
from jax.sharding import PartitionSpec as P

EPS = 1e-06
DELIVER = 4
CHIPS = 32
NY, NZ = 4, 8
TOK = 128
NH = 16
DH = 128
HALF = NH // 2
CHUNKS = 4
CH = HALF // CHUNKS
ROWS = CH * DH // CHIPS
SPLIT = NZ // CH
ROW_WIDTH = 64 * DH
MESH = pl.DeviceIdType.MESH
F32 = jnp.float32
BF16 = jnp.bfloat16


def mm(left, right, lc, rc):
    return lax.dot_general(
        left, right, (((lc,), (rc,)), ((), ())), preferred_element_type=F32
    )


def kernel(
    q_hbm, k_hbm, v_hbm, g_hbm,
    n_out, qg_out, kg_out, vg_out,
    q_in, k_in, v_in, g_in,
    flat_a, flat_b, qh, kh, vh, gh, wts, att, full, agr, prior, kg_acc, vg_acc,
    given, state, sib, share, other, base,
    mine, theirs, got, joint, owned, bases, early, relay, lent,
    acc, msg, sums,
    load_sem, d2d_send, d2d_recv, pair_send, pair_recv, far_send, far_recv, x_send, x_recv,
):
    seq, head = lax.axis_index("seq"), lax.axis_index("head")
    s, c = seq // 2, lax.rem(seq, 2)
    oc = 1 - c

    loads = [
        pltpu.make_async_copy(src, dst, load_sem.at[i])
        for i, (src, dst) in enumerate(
            ((k_hbm, k_in), (v_hbm, v_in), (q_hbm, q_in), (g_hbm, g_in))
        )
    ]
    for ld in loads:
        ld.start()

    y, z = s // NZ, lax.rem(s, NZ)
    odd = lax.rem(z, 2)
    sign = 2 * odd - 1
    mate = z - sign

    def at(yy, zz):
        return ((yy * NZ + zz) * 2 + c, head)

    def ring(zz):
        return lax.rem(zz + NZ, NZ)

    bar = pltpu.get_barrier_semaphore()
    peers = [(2 * s + oc, head), at(y, mate)]
    peers += [(seq, lax.rem(head + i, 4)) for i in range(1, 4)]
    peers += [
        at(lax.rem(y + dy, NY), ring(z + sign * w))
        for w in (0, 1, 2, 3, -2)
        for dy in range(NY)
        if w or dy
    ]
    for peer in peers:
        pl.semaphore_signal(bar, inc=1, device_id=peer, device_id_type=MESH)

    def flatten(src, flat):
        flat[...] = src[...].astype(F32).reshape(TOK * NH, DH)

    def pick(flat, h):
        return flat[pl.ds(h, TOK, stride=NH), :].astype(BF16)

    def over(body):
        def step(i, _):
            body([4 * i + u for u in range(4)])
            return 0

        lax.fori_loop(0, NH // 4, step, 0)

    rows = lax.broadcasted_iota(jnp.int32, (TOK, TOK), 0)
    cols = lax.broadcasted_iota(jnp.int32, (TOK, TOK), 1)
    causal = cols <= rows

    def copy(sems, k, src, dst, to):
        return pltpu.make_async_remote_copy(
            src_ref=src, dst_ref=dst, send_sem=sems[0].at[k], recv_sem=sems[1].at[k],
            device_id=to, device_id_type=MESH,
        )

    d2d_sems, pair_sems, far_sems = (d2d_send, d2d_recv), (pair_send, pair_recv), (far_send, far_recv)

    def d2d_up(j, n):
        return copy(d2d_sems, (j, 0, n), given.at[j, n], sib.at[j, n], peers[0])

    def d2d_down(j, n, part):
        return copy(
            d2d_sems, (j, 1 + part, n), share.at[j, n, pl.ds(4 * part, 4)],
            other.at[j, n, pl.ds(4 * part, 4)], peers[0],
        )

    def pair_up(j, n):
        return copy(pair_sems, (j, 0, n), theirs.at[j, n], got.at[j, n], peers[1])

    def pair_down(j, n):
        return copy(pair_sems, (j, 1, n), relay.at[j, n], lent.at[j, n], peers[1])

    def far(j, way, n):
        return copy(
            far_sems, (j, way, n), joint.at[j, n, pl.ds(0, 15)], owned.at[j, n, pl.ds(0, 15)], peers[1]
        )

    FAR = [(w, dy) for w in (3, 2, 1, 0) for dy in (2, 1, 3, 0) if w or dy]

    def slot_z(f):
        return ring(z + sign * f) if f < 4 else ring(mate - sign * (f - 4))

    def slot_of(zo):
        t = ring(sign * (zo - z))
        return jnp.where(t < 4, t, 11 - t)

    def put_state(ref, j, n, i, value):
        ref[j, n, pl.ds(i * SPLIT, SPLIT)] = value.reshape(SPLIT, NY * ROWS, DH)

    def head_of(ref, j, n, i):
        blocks = [ref[j, n, slot_of(i * SPLIT + u)] for u in range(SPLIT)]
        return jnp.concatenate(blocks, axis=0).astype(BF16)

    def scan(j, make, during_up, during_down, use, reverse):
        def theirs_of(n):
            return [oc * HALF + n * CH + i for i in range(CH)]

        def own_of(n):
            return [c * HALF + n * CH + i for i in range(CH)]

        def give(n):
            made = make(theirs_of(n) + own_of(n))
            for i in range(CH):
                put_state(given, j, n, i, made[i])
                put_state(state, j, n, i, made[CH + i])
            if j == 0 and n == 0:
                pl.semaphore_wait(bar, len(peers))
            d2d_up(j, n).start()

        def send_pair(n):
            d2d_up(j, n).wait_recv()
            for f in range(NZ):
                zo = slot_z(f)
                total = (state[j, n, zo] + sib[j, n, zo]).reshape(NY, ROWS, DH)
                ref = mine if f < 4 else theirs
                ref[j, n, pl.ds(f % 4 * NY, NY)] = total
            pair_up(j, n).start()

        def send_up(n):
            pair_up(j, n).wait_recv()
            joint[j, n] = mine[j, n] + got[j, n]
            for w, dy in FAR:
                yo = lax.rem(y + dy, NY)
                copy(
                    far_sems, (j, 0, n), joint.at[j, n, w * NY + yo], owned.at[j, n, y * 4 + z // 2],
                    at(yo, ring(z + sign * w)),
                ).start()
            owned[j, n, y * 4 + z // 2] = joint[j, n, y]

        def send_down(n):
            far(j, 0, n).wait_recv()
            run = jnp.zeros((ROWS, DH), F32)
            for t in range(15, -1, -1) if reverse else range(16):
                bases[j, n, t] = run
                run = run + owned[j, n, t]
            for w, dy in FAR:
                yr = lax.rem(y + dy, NY)
                zr = ring(z + w - 2 * w * lax.rem(z + w, 2))
                copy(
                    far_sems, (j, 1, n), bases.at[j, n, yr * 4 + zr // 2], early.at[j, n, w * NY + y],
                    at(yr, zr),
                ).start()
            early[j, n, y] = bases[j, n, y * 4 + z // 2]

        chip_first = 1 - odd if reverse else odd
        first = oc if reverse else c

        def settle(n, part, values):
            for w in range(4):
                f = 4 * part + w
                zo = slot_z(f)
                value = values[w * NY : (w + 1) * NY].reshape(NY * ROWS, DH)
                share[j, n, f] = value + jnp.where(first == 0, state[j, n, zo], 0.0)
                base[j, n, f] = value + jnp.where(first == 1, sib[j, n, zo], 0.0)
            d2d_down(j, n, part).start()

        def send_mate(n):
            far(j, 1, n).wait_recv()
            before = early[j, n]
            relay[j, n] = before + jnp.where(chip_first == 0, mine[j, n], 0.0)
            pair_down(j, n).start()
            settle(n, 0, before + jnp.where(chip_first == 1, got[j, n], 0.0))

        def finish_chunk(n):
            heads, states = [], []
            if n < CHUNKS:
                pair_down(j, n).wait_recv()
                settle(n, 1, lent[j, n])
                heads += own_of(n)
                states += [head_of(base, j, n, i) for i in range(CH)]
            if n:
                d2d_down(j, n - 1, 0).wait_recv()
                d2d_down(j, n - 1, 1).wait_recv()
                heads += theirs_of(n - 1)
                states += [head_of(other, j, n - 1, i) for i in range(CH)]
            use(heads, states)

        for n in range(CHUNKS + 2):
            if n < CHUNKS:
                give(n)
            if 0 <= n - 1 < CHUNKS:
                send_pair(n - 1)
            if n >= 2:
                send_up(n - 2)
        during_up()
        for n in range(CHUNKS):
            send_down(n)
        during_down()
        for n in range(CHUNKS):
            send_mate(n)
        for n in range(CHUNKS + 1):
            finish_chunk(n)

    def scan_end(j):
        for n in range(CHUNKS):
            d2d_up(j, n).wait_send()
            d2d_down(j, n, 0).wait_send()
            d2d_down(j, n, 1).wait_send()
            pair_up(j, n).wait_send()
            pair_down(j, n).wait_send()
            far(j, 0, n).wait_send()
            far(j, 1, n).wait_send()

    loads[0].wait()
    flatten(k_in, flat_a)
    loads[1].wait()
    flatten(v_in, flat_b)

    def make_state(heads):
        kv = [(pick(flat_a, h), pick(flat_b, h)) for h in heads]
        for h, (kk, vv) in zip(heads, kv):
            kh[h], vh[h] = kk, vv
        return [mm(kk, vv, 0, 0) for kk, vv in kv]

    def local_attention():
        loads[2].wait()
        flatten(q_in, flat_a)

        def body(heads):
            qs = [pick(flat_a, h) for h in heads]
            ws = [jnp.where(causal, mm(qq, kh[h], 1, 1), 0.0).astype(BF16) for h, qq in zip(heads, qs)]
            outs = [mm(w, vh[h], 1, 0) for h, w in zip(heads, ws)]
            for h, qq, w, o in zip(heads, qs, ws, outs):
                qh[h] = qq
                wts[h] = w
                att[h] = o

        over(body)

    def load_grads():
        loads[3].wait()
        flatten(g_in, flat_b)

        def body(heads):
            gs = [pick(flat_b, h) for h in heads]
            for h, gg in zip(heads, gs):
                gh[h] = gg

        over(body)
        acc[...] = jnp.zeros_like(acc)

    def attend(heads, priors):
        parts = [att[h] + mm(qh[h], pr, 1, 0) for h, pr in zip(heads, priors)]
        grads = [gh[h].astype(F32) for h in heads]
        for h, pr, a in zip(heads, priors, parts):
            prior[h] = pr
            full[h] = a
        acc[0] += sum(a * a for a in parts)
        acc[1] += sum(a * g for a, g in zip(parts, grads))

    scan(0, make_state, local_attention, load_grads, attend, False)

    sq = jnp.sum(acc[0], axis=1, keepdims=True)
    dt = jnp.sum(acc[1], axis=1, keepdims=True)
    packed = jnp.where(cols == 0, sq, jnp.where(cols == 1, dt, 0.0))
    msg[...] = jnp.transpose(packed)[0:8]
    xs = [
        pltpu.make_async_remote_copy(
            src_ref=msg, dst_ref=sums.at[i], send_sem=x_send.at[i], recv_sem=x_recv.at[i],
            device_id=(seq, lax.rem(head + i + 1, 4)), device_id_type=MESH,
        )
        for i in range(3)
    ]
    for x in xs:
        x.start()
    for x in xs:
        x.wait_recv()
    total = msg[...] + sums[0] + sums[1] + sums[2]
    inv = 1.0 / jnp.sqrt(total[0:1] / ROW_WIDTH + EPS)
    fac = inv * inv * inv * total[1:2] / ROW_WIDTH
    both = jnp.transpose(jnp.where(rows == 0, inv, jnp.where(rows == 1, fac, 0.0)))
    inv_col, fac_col = both[:, 0:1], both[:, 1:2]

    def make_grad(heads):
        ags = [(inv_col * gh[h].astype(F32) - full[h] * fac_col).astype(BF16) for h in heads]
        for h, ag in zip(heads, ags):
            agr[h] = ag
        return [mm(qh[h], ag, 0, 0) for h, ag in zip(heads, ags)]

    def query_side():
        def body(heads):
            ags = [agr[h] for h in heads]
            ms = [jnp.where(causal, mm(ag, vh[h], 1, 1), 0.0).astype(BF16) for h, ag in zip(heads, ags)]
            qgs = [
                mm(m, kh[h], 1, 0) + mm(ag, prior[h], 1, 1) for h, m, ag in zip(heads, ms, ags)
            ]
            kgs = [mm(m, qh[h], 0, 0) for h, m in zip(heads, ms)]
            vgs = [mm(wts[h], ag, 0, 0) for h, ag in zip(heads, ags)]
            normed = [full[h] * inv_col for h in heads]
            for i, h in enumerate(heads):
                flat_a[pl.ds(h, TOK, stride=NH), :] = qgs[i]
                flat_b[pl.ds(h, TOK, stride=NH), :] = normed[i]
                kg_acc[h] = kgs[i]
                vg_acc[h] = vgs[i]

        over(body)

    def emit(flat, ref):
        ref[...] = flat[...].reshape(TOK, NH, DH).astype(BF16)

    def write_two():
        emit(flat_b, n_out)
        emit(flat_a, qg_out)

    def finish(heads, laters):
        keys = [kg_acc[h] + mm(vh[h], lt, 1, 1) for h, lt in zip(heads, laters)]
        values = [vg_acc[h] + mm(kh[h], lt, 1, 0) for h, lt in zip(heads, laters)]
        for h, kg, vg in zip(heads, keys, values):
            flat_a[pl.ds(h, TOK, stride=NH), :] = kg
            flat_b[pl.ds(h, TOK, stride=NH), :] = vg

    scan(1, make_grad, query_side, write_two, finish, True)
    emit(flat_a, kg_out)
    emit(flat_b, vg_out)

    scan_end(0)
    scan_end(1)
    for x in xs:
        x.wait_send()


def deliver(*refs):
    sem = refs[8]
    copies = [pltpu.make_async_copy(refs[i], refs[4 + i], sem.at[i]) for i in range(4)]
    for cp in copies:
        cp.start()
    for cp in copies:
        cp.wait()


def shards(queries, keys, values, out_grad):
    shape = (TOK, NH, DH)
    half = (2, CHUNKS, NZ, NY * ROWS, DH)
    part = (2, CHUNKS, 16, ROWS, DH)
    per = (2, 2, CHUNKS)
    vm = pltpu.VMEM
    dma = pltpu.SemaphoreType.DMA
    hm = (NH, TOK, DH)
    results = pl.pallas_call(
        kernel,
        out_shape=[jax.ShapeDtypeStruct(shape, BF16)] * 4,
        in_specs=[pl.BlockSpec(memory_space=pltpu.HBM)] * 4,
        out_specs=[pl.BlockSpec(memory_space=pltpu.VMEM)] * 4,
        scratch_shapes=[vm(shape, BF16)] * 4
        + [vm((TOK * NH, DH), F32)] * 2
        + [vm(hm, BF16)] * 5
        + [vm(hm, F32), vm(hm, F32), vm(hm, BF16), vm(hm, BF16), vm(hm, F32), vm(hm, F32)]
        + [vm(half, F32)] * 6
        + [vm(part, F32)] * 9
        + [vm((2, TOK, DH), F32), vm((8, TOK), F32), vm((3, 8, TOK), F32)]
        + [dma((4,)), dma((2, 3, CHUNKS)), dma((2, 3, CHUNKS)), dma(per), dma(per), dma(per), dma(per)]
        + [dma((3,)), dma((3,))],
        compiler_params=pltpu.CompilerParams(
            collective_id=0, has_side_effects=True, vmem_limit_bytes=48 << 20
        ),
    )(*[pltpu.with_memory_space_constraint(x, pltpu.HBM) for x in (queries, keys, values, out_grad)])
    block = pl.BlockSpec((TOK // DELIVER, NH, DH), lambda i: (i, 0, 0))
    return pl.pallas_call(
        deliver,
        out_shape=[jax.ShapeDtypeStruct(shape, BF16)] * 4,
        in_specs=[pl.BlockSpec(memory_space=pltpu.VMEM)] * 4,
        out_specs=[pl.BlockSpec(memory_space=pl.ANY)] * 4,
        scratch_shapes=[dma((4,))],
        compiler_params=pltpu.CompilerParams(vmem_limit_bytes=8 << 20),
    )(*results)


def solution(mesh):
    spec = P("seq", "head", None)
    return jax.shard_map(
        shards, mesh=mesh, in_specs=(spec,) * 4, out_specs=(spec,) * 4, check_vma=False
    )
```

```python
import jax
import jax.numpy as jnp
from jax import lax
from jax.experimental import pallas as pl
from jax.experimental.pallas import tpu as pltpu
from jax.sharding import PartitionSpec as P

EPS = 1e-06
CHIPS = 32
NY, NZ = 4, 8
TOK = 128
NH = 16
DH = 128
HALF = NH // 2
CHUNKS = 4
CH = HALF // CHUNKS
ROWS = CH * DH // CHIPS
SPLIT = NZ // CH
ROW_WIDTH = 64 * DH
MESH = pl.DeviceIdType.MESH
FORWARD_FILL = {"start": (0, 1), "down1": (2,), "down3": (3, 4, 5)}
BACKWARD_FILL = {"start": (0,), "down1": (1, 2), "down3": (3, 4), "mate3": (5,)}
F32 = jnp.float32
BF16 = jnp.bfloat16


def mm(left, right, lc, rc):
    return lax.dot_general(
        left, right, (((lc,), (rc,)), ((), ())), preferred_element_type=F32
    )


def kernel(
    q_hbm, k_hbm, v_hbm, g_hbm,
    n_out, qg_out, kg_out, vg_out,
    q_in, k_in, v_in, g_in,
    flat_a, flat_b, qh, kh, vh, gh, wts, agr, prior, att, full, kg_acc, vg_acc,
    lend, borrow, give_back, take_back, given, base, state,
    mine, theirs, got, joint, owned, bases, early, relay, lent,
    acc, msg, sums,
    load_sem, d2d_send, d2d_recv, pair_send, pair_recv, far_send, far_recv, x_send, x_recv,
):
    seq, head = lax.axis_index("seq"), lax.axis_index("head")
    s, c = seq // 2, lax.rem(seq, 2)
    oc = 1 - c

    loads = [
        pltpu.make_async_copy(src, dst, load_sem.at[i])
        for i, (src, dst) in enumerate(
            ((k_hbm, k_in), (v_hbm, v_in), (q_hbm, q_in), (g_hbm, g_in))
        )
    ]
    for ld in loads:
        ld.start()

    y, z = s // NZ, lax.rem(s, NZ)
    odd = lax.rem(z, 2)
    sign = 2 * odd - 1
    mate = z - sign

    def at(yy, zz):
        return ((yy * NZ + zz) * 2 + c, head)

    def ring(zz):
        return lax.rem(zz + NZ, NZ)

    bar = pltpu.get_barrier_semaphore()
    sibling, partner = (2 * s + oc, head), at(y, mate)
    sum_peers = [sibling] + [
        (2 * s + cc, lax.rem(head + i, 4)) for i in range(1, 4) for cc in (c, oc)
    ]
    peers = sum_peers + [partner]
    peers += [
        at(lax.rem(y + dy, NY), ring(z + sign * w))
        for w in (0, 1, 2, 3, -2)
        for dy in range(NY)
        if w or dy
    ]
    for peer in peers:
        pl.semaphore_signal(bar, inc=1, device_id=peer, device_id_type=MESH)

    def flatten(src, flat):
        flat[...] = src[...].astype(F32).reshape(TOK * NH, DH)

    def pick(flat, h):
        return flat[pl.ds(h, TOK, stride=NH), :]

    def place(flat, h, value):
        flat[pl.ds(h, TOK, stride=NH), :] = value

    def by_four(body):
        def step(i, _):
            body([4 * i + u for u in range(4)])
            return 0

        lax.fori_loop(0, HALF // 4, step, 0)

    rows = lax.broadcasted_iota(jnp.int32, (TOK, TOK), 0)
    cols = lax.broadcasted_iota(jnp.int32, (TOK, TOK), 1)
    causal = cols <= rows

    def copy(sems, k, src, dst, to):
        return pltpu.make_async_remote_copy(
            src_ref=src, dst_ref=dst, send_sem=sems[0].at[k], recv_sem=sems[1].at[k],
            device_id=to, device_id_type=MESH,
        )

    d2d_sems, pair_sems, far_sems = (d2d_send, d2d_recv), (pair_send, pair_recv), (far_send, far_recv)

    def state_swap(n):
        return copy(d2d_sems, n, given.at[n], state.at[0, c, n], sibling)

    def state_swap_wait(n):
        return copy(d2d_sems, n, given.at[n], state.at[0, oc, n], sibling)

    def lending(i):
        return copy(d2d_sems, CHUNKS + i, lend.at[i], borrow.at[i], sibling)

    def returning(i):
        return copy(d2d_sems, CHUNKS + 4 + i, give_back.at[i], take_back.at[i], sibling)

    def returning_part(i, n):
        part = pl.ds(n * CH, CH)
        return copy(
            d2d_sems, CHUNKS + 4 + 2 * (n + 1) + i - 2, give_back.at[i, part], take_back.at[i, part], sibling
        )

    def pair_up(j, n):
        return copy(pair_sems, (j, 0, n), theirs.at[j, n], got.at[j, n], partner)

    def pair_down(j, n):
        return copy(pair_sems, (j, 1, n), relay.at[j, n], lent.at[j, n], partner)

    def far(j, way, n):
        return copy(
            far_sems, (j, way, n), joint.at[j, n, pl.ds(0, 15)], owned.at[j, n, pl.ds(0, 15)], partner
        )

    FAR = [(w, dy) for w in (3, 2, 1, 0) for dy in (2, 1, 3, 0) if w or dy]

    def slot_z(f):
        return ring(z + sign * f) if f < 4 else ring(mate - sign * (f - 4))

    def slot_of(zo):
        t = ring(sign * (zo - z))
        return jnp.where(t < 4, t, 11 - t)

    def cut(value):
        return value.reshape(SPLIT, NY * ROWS, DH)

    def state_of(j, b, n, i):
        return state[j, b, n, pl.ds(i * SPLIT, SPLIT)].reshape(DH, DH)

    def base_of(n, i):
        return jnp.concatenate([base[n, slot_of(i * SPLIT + u)] for u in range(SPLIT)], axis=0)

    def scan(j, make, fill, use, reverse):
        def send_pair(n):
            if j == 0:
                state_swap_wait(n).wait_recv()
            for f in range(NZ):
                zo = slot_z(f)
                total = (state[j, 0, n, zo] + state[j, 1, n, zo]).reshape(NY, ROWS, DH)
                ref = mine if f < 4 else theirs
                ref[j, n, pl.ds(f % 4 * NY, NY)] = total
            pair_up(j, n).start()

        def send_up(n):
            pair_up(j, n).wait_recv()
            joint[j, n] = mine[j, n] + got[j, n]
            for w, dy in FAR:
                yo = lax.rem(y + dy, NY)
                copy(
                    far_sems, (j, 0, n), joint.at[j, n, w * NY + yo], owned.at[j, n, y * 4 + z // 2],
                    at(yo, ring(z + sign * w)),
                ).start()
            owned[j, n, y * 4 + z // 2] = joint[j, n, y]

        def send_down(n):
            far(j, 0, n).wait_recv()
            run = jnp.zeros((ROWS, DH), F32)
            for t in range(15, -1, -1) if reverse else range(16):
                bases[j, n, t] = run
                run = run + owned[j, n, t]
            for w, dy in FAR:
                yr = lax.rem(y + dy, NY)
                zr = ring(z + w - 2 * w * lax.rem(z + w, 2))
                copy(
                    far_sems, (j, 1, n), bases.at[j, n, yr * 4 + zr // 2], early.at[j, n, w * NY + y],
                    at(yr, zr),
                ).start()
            early[j, n, y] = bases[j, n, y * 4 + z // 2]

        chip_first = 1 - odd if reverse else odd

        def send_mate(n):
            far(j, 1, n).wait_recv()
            before = early[j, n]
            relay[j, n] = before + jnp.where(chip_first == 0, mine[j, n], 0.0)
            pair_down(j, n).start()
            own = before + jnp.where(chip_first == 1, got[j, n], 0.0)
            base[n, pl.ds(0, 4)] = own.reshape(4, NY * ROWS, DH)

        def finish_chunk(n):
            pair_down(j, n).wait_recv()
            base[n, pl.ds(4, 4)] = lent[j, n].reshape(4, NY * ROWS, DH)
            heads = [n * CH + i for i in range(CH)]
            first = [base_of(n, i) for i in range(CH)]
            block = 1 if reverse else 0
            second = [f + state_of(j, block, n, i) for i, f in enumerate(first)]
            first, second = [[x.astype(BF16) for x in xs] for xs in (first, second)]
            use(n, heads, *((second, first) if reverse else (first, second)))

        for n in range(CHUNKS + 2):
            if n < CHUNKS:
                make(n)
            if 0 <= n - 1 < CHUNKS:
                send_pair(n - 1)
            if n >= 2:
                send_up(n - 2)
        fill("start")
        for n in range(CHUNKS):
            send_down(n)
            fill("down%d" % n)
        for n in range(CHUNKS):
            send_mate(n)
            fill("mate%d" % n)
        for n in range(CHUNKS):
            finish_chunk(n)

    def scan_end(j):
        for n in range(CHUNKS):
            pair_up(j, n).wait_send()
            pair_down(j, n).wait_send()
            far(j, 0, n).wait_send()
            far(j, 1, n).wait_send()

    loads[0].wait()
    flatten(k_in, flat_a)
    loads[1].wait()
    flatten(v_in, flat_b)

    def make_state(n):
        span = range(n * CH, n * CH + CH)
        away = [(pick(flat_a, oc * HALF + i), pick(flat_b, oc * HALF + i)) for i in span]
        here = [(pick(flat_a, c * HALF + i), pick(flat_b, c * HALF + i)) for i in span]
        states = [mm(kk.astype(BF16), vv.astype(BF16), 0, 0) for kk, vv in away + here]
        for u, i in enumerate(span):
            lend[0, i], lend[1, i] = away[u]
            kk, vv = here[u]
            kh[c * HALF + i] = kk.astype(BF16)
            vh[c * HALF + i] = vv.astype(BF16)
            given[n, pl.ds(u * SPLIT, SPLIT)] = cut(states[u])
            state[0, c, n, pl.ds(u * SPLIT, SPLIT)] = cut(states[CH + u])
        if n == 0:
            pl.semaphore_wait(bar, len(peers))
        state_swap(n).start()

    def share(index, flat, ref):
        def body(heads):
            away = [pick(flat, oc * HALF + i) for i in heads]
            here = [pick(flat, c * HALF + i).astype(BF16) for i in heads]
            for i, x, m in zip(heads, away, here):
                lend[index, i] = x
                ref[c * HALF + i] = m

        by_four(body)
        lending(index).start()

    def receive(index, ref):
        lending(index).wait_recv()

        def body(heads):
            for i in heads:
                ref[oc * HALF + i] = borrow[index, i].astype(BF16)

        by_four(body)

    def local_attention(b):
        def body(heads):
            hs = [b * HALF + i for i in heads]
            ws = [jnp.where(causal, mm(qh[h], kh[h], 1, 1), 0.0).astype(BF16) for h in hs]
            outs = [mm(w, vh[h], 1, 0) for h, w in zip(hs, ws)]
            for h, w, o in zip(hs, ws, outs):
                wts[h] = w
                att[h] = o

        by_four(body)

    def lend_query():
        lending(0).start()
        lending(1).start()
        loads[2].wait()
        flatten(q_in, flat_a)
        share(2, flat_a, qh)

    def lend_grad():
        loads[3].wait()
        flatten(g_in, flat_b)
        share(3, flat_b, gh)

    def borrow_three():
        receive(0, kh)
        receive(1, vh)
        receive(2, qh)

    def borrow_grad():
        receive(3, gh)
        acc[...] = jnp.zeros_like(acc)

    forward_work = [
        lend_query, lend_grad, lambda: local_attention(c), borrow_three, lambda: local_attention(oc),
        borrow_grad,
    ]

    def fill_forward(place_name):
        for task in FORWARD_FILL.get(place_name, ()):
            forward_work[task]()

    def attend(n, heads, *priors):
        for b in range(2):
            hs = [b * HALF + i for i in heads]
            parts = [att[h] + mm(qh[h], pr, 1, 0) for h, pr in zip(hs, priors[b])]
            grads = [gh[h].astype(F32) for h in hs]
            for h, pr, a in zip(hs, priors[b], parts):
                prior[h] = pr
                full[h] = a
            acc[b, 0] += sum(a * a for a in parts)
            acc[b, 1] += sum(a * g for a, g in zip(parts, grads))

    scan(0, make_state, fill_forward, attend, False)

    packed = jnp.zeros((TOK, TOK), F32)
    for b in range(2):
        for i in range(2):
            packed = jnp.where(cols == 2 * b + i, jnp.sum(acc[b, i], axis=1, keepdims=True), packed)
    msg[...] = jnp.transpose(packed)[0:8]
    xs = [
        copy((x_send, x_recv), i, msg, sums.at[i], peer) for i, peer in enumerate(sum_peers)
    ]
    for x in xs:
        x.start()
    for x in xs:
        x.wait_recv()
    total = msg[...]
    for i in range(len(xs)):
        total = total + sums[i]
    back = jnp.zeros((TOK, TOK), F32)
    for b in range(2):
        inv = 1.0 / jnp.sqrt(total[2 * b : 2 * b + 1] / ROW_WIDTH + EPS)
        fac = inv * inv * inv * total[2 * b + 1 : 2 * b + 2] / ROW_WIDTH
        back = jnp.where(rows == 2 * b, inv, jnp.where(rows == 2 * b + 1, fac, back))
    back = jnp.transpose(back)
    inv_col = [back[:, 0:1], back[:, 2:3]]
    fac_col = [back[:, 1:2], back[:, 3:4]]

    def make_grad(n):
        span = range(n * CH, n * CH + CH)
        where = [(b, u, b * HALF + i) for b in range(2) for u, i in enumerate(span)]
        ags = [
            (inv_col[b] * gh[h].astype(F32) - full[h] * fac_col[b]).astype(BF16) for b, _, h in where
        ]
        states = [mm(qh[h], ag, 0, 0) for (_, _, h), ag in zip(where, ags)]
        for (b, u, h), ag, st in zip(where, ags, states):
            agr[h] = ag
            state[1, b, n, pl.ds(u * SPLIT, SPLIT)] = cut(st)

    def query_side(b, start, keep):
        scale = jnp.where(b == 0, inv_col[0], inv_col[1])

        def body(heads):
            hs = [b * HALF + i for i in heads]
            ags = [agr[h] for h in hs]
            ms = [jnp.where(causal, mm(ag, vh[h], 1, 1), 0.0).astype(BF16) for h, ag in zip(hs, ags)]
            qgs = [mm(m, kh[h], 1, 0) + mm(ag, prior[h], 1, 1) for h, m, ag in zip(hs, ms, ags)]
            kgs = [mm(m, qh[h], 0, 0) for h, m in zip(hs, ms)]
            vgs = [mm(wts[h], ag, 0, 0) for h, ag in zip(hs, ags)]
            normed = [full[h] * scale for h in hs]
            for u, i in enumerate(heads):
                keep(i, normed[u], qgs[u])
                kg_acc[hs[u]] = kgs[u]
                vg_acc[hs[u]] = vgs[u]

        body([start + u for u in range(4)])

    def keep_away(i, left, right):
        give_back[0, i] = left
        give_back[1, i] = right

    def keep_here(i, left, right):
        place(flat_a, c * HALF + i, left)
        place(flat_b, c * HALF + i, right)

    def emit(flat, ref):
        ref[...] = flat[...].reshape(TOK, NH, DH).astype(BF16)

    def give_two():
        returning(0).start()
        returning(1).start()

    def write_two():
        returning(0).wait_recv()
        returning(1).wait_recv()

        def body(heads):
            for i in heads:
                place(flat_a, oc * HALF + i, take_back[0, i])
                place(flat_b, oc * HALF + i, take_back[1, i])

        by_four(body)
        emit(flat_a, n_out)
        emit(flat_b, qg_out)

    backward_work = [
        lambda: query_side(oc, 0, keep_away), lambda: query_side(oc, 4, keep_away), give_two,
        lambda: query_side(c, 0, keep_here), lambda: query_side(c, 4, keep_here), write_two,
    ]

    def fill_backward(place_name):
        for task in BACKWARD_FILL.get(place_name, ()):
            backward_work[task]()

    def collect(n):
        for i in range(2):
            returning_part(2 + i, n).wait_recv()
        for i in range(n * CH, n * CH + CH):
            place(flat_a, oc * HALF + i, take_back[2, i])
            place(flat_b, oc * HALF + i, take_back[3, i])

    def finish(n, heads, *laters):
        def grads(b):
            hs = [b * HALF + i for i in heads]
            lts = [jnp.where(b == 0, l0, l1) for l0, l1 in zip(*laters)]
            keys = [kg_acc[h] + mm(vh[h], lt, 1, 1) for h, lt in zip(hs, lts)]
            values = [vg_acc[h] + mm(kh[h], lt, 1, 0) for h, lt in zip(hs, lts)]
            return keys, values

        for i, kg, vg in zip(heads, *grads(oc)):
            give_back[2, i] = kg
            give_back[3, i] = vg
        for i in range(2):
            returning_part(2 + i, n).start()
        for i, kg, vg in zip(heads, *grads(c)):
            keep_here(i, kg, vg)
        if n:
            collect(n - 1)

    scan(1, make_grad, fill_backward, finish, True)
    collect(CHUNKS - 1)
    emit(flat_a, kg_out)
    emit(flat_b, vg_out)

    for n in range(CHUNKS):
        state_swap(n).wait_send()
        for i in range(2):
            returning_part(2 + i, n).wait_send()
    for i in range(4):
        lending(i).wait_send()
    for i in range(2):
        returning(i).wait_send()
    scan_end(0)
    scan_end(1)
    for x in xs:
        x.wait_send()


def deliver(*refs):
    sem = refs[8]
    copies = [pltpu.make_async_copy(refs[i], refs[4 + i], sem.at[i]) for i in range(4)]
    for cp in copies:
        cp.start()
    for cp in copies:
        cp.wait()


def shards(queries, keys, values, out_grad):
    shape = (TOK, NH, DH)
    half = (CHUNKS, NZ, NY * ROWS, DH)
    part = (2, CHUNKS, 16, ROWS, DH)
    per = (2, 2, CHUNKS)
    vm = pltpu.VMEM
    dma = pltpu.SemaphoreType.DMA
    hm = (NH, TOK, DH)
    swap = (4, HALF, TOK, DH)
    d2d = 4 + 4 + 3 * CHUNKS
    results = pl.pallas_call(
        kernel,
        out_shape=[jax.ShapeDtypeStruct(shape, BF16)] * 4,
        in_specs=[pl.BlockSpec(memory_space=pltpu.HBM)] * 4,
        out_specs=[pl.BlockSpec(memory_space=pltpu.VMEM)] * 4,
        scratch_shapes=[vm(shape, BF16)] * 4
        + [vm((TOK * NH, DH), F32)] * 2
        + [vm(hm, BF16)] * 7
        + [vm(hm, F32)] * 4
        + [vm(swap, F32)] * 4
        + [vm(half, F32)] * 2
        + [vm((2, 2) + half, F32)]
        + [vm(part, F32)] * 9
        + [vm((2, 2, TOK, DH), F32), vm((8, TOK), F32), vm((7, 8, TOK), F32)]
        + [dma((4,)), dma((d2d,)), dma((d2d,)), dma(per), dma(per), dma(per), dma(per)]
        + [dma((7,)), dma((7,))],
        compiler_params=pltpu.CompilerParams(
            collective_id=0, has_side_effects=True, vmem_limit_bytes=48 << 20
        ),
    )(*[pltpu.with_memory_space_constraint(x, pltpu.HBM) for x in (queries, keys, values, out_grad)])
    return pl.pallas_call(
        deliver,
        out_shape=[jax.ShapeDtypeStruct(shape, BF16)] * 4,
        in_specs=[pl.BlockSpec(memory_space=pltpu.VMEM)] * 4,
        out_specs=[pl.BlockSpec(memory_space=pl.ANY)] * 4,
        scratch_shapes=[dma((4,))],
        compiler_params=pltpu.CompilerParams(vmem_limit_bytes=8 << 20),
    )(*results)


def solution(mesh):
    spec = P("seq", "head", None)
    return jax.shard_map(
        shards, mesh=mesh, in_specs=(spec,) * 4, out_specs=(spec,) * 4, check_vma=False
    )
```

```python
import jax
import jax.numpy as jnp
from jax import lax
from jax.experimental import pallas as pl
from jax.experimental.pallas import tpu as pltpu
from jax.sharding import PartitionSpec as P

EPS = 1e-06
CHIPS = 32
NY, NZ = 4, 8
TOK = 128
NH = 16
DH = 128
HALF = NH // 2
CHUNKS = 4
CH = HALF // CHUNKS
ROWS = CH * DH // CHIPS
SPLIT = NZ // CH
ROW_WIDTH = 64 * DH
MESH = pl.DeviceIdType.MESH
FORWARD_FILL = {"start": (0, 1), "down1": (2,), "down3": (3, 4, 5)}
BACKWARD_FILL = {"start": (0, 1, 2), "down3": (3, 4), "mate3": (5,)}
F32 = jnp.float32
BF16 = jnp.bfloat16


def mm(left, right, lc, rc):
    return lax.dot_general(
        left, right, (((lc,), (rc,)), ((), ())), preferred_element_type=F32
    )


def kernel(
    q_hbm, k_hbm, v_hbm, g_hbm,
    n_out, qg_out, kg_out, vg_out,
    q_in, k_in, v_in, g_in,
    flat_a, flat_b, qh, kh, vh, gh, wts, agr, prior, att, full, kg_acc, vg_acc,
    lend, borrow, give_back, take_back, given, base, state,
    mine, theirs, got, joint, owned, bases, early, relay, lent,
    acc, msg, sums,
    load_sem, d2d_send, d2d_recv, pair_send, pair_recv, far_send, far_recv, x_send, x_recv,
):
    seq, head = lax.axis_index("seq"), lax.axis_index("head")
    s, c = seq // 2, lax.rem(seq, 2)
    oc = 1 - c

    loads = [
        pltpu.make_async_copy(src, dst, load_sem.at[i])
        for i, (src, dst) in enumerate(
            ((k_hbm, k_in), (v_hbm, v_in), (q_hbm, q_in), (g_hbm, g_in))
        )
    ]
    for ld in loads:
        ld.start()

    y, z = s // NZ, lax.rem(s, NZ)
    odd = lax.rem(z, 2)
    sign = 2 * odd - 1
    mate = z - sign

    def at(yy, zz):
        return ((yy * NZ + zz) * 2 + c, head)

    def ring(zz):
        return lax.rem(zz + NZ, NZ)

    bar = pltpu.get_barrier_semaphore()
    sibling, partner = (2 * s + oc, head), at(y, mate)
    sum_peers = [sibling] + [
        (2 * s + cc, lax.rem(head + i, 4)) for i in range(1, 4) for cc in (c, oc)
    ]
    far_off = sorted(
        [(w, dy) for w in (0, 1, 2, 3, -2) for dy in range(NY) if w or dy],
        key=lambda o: -(abs(o[0]) + min(o[1], NY - o[1])),
    )
    peers = [at(lax.rem(y + dy, NY), ring(z + sign * w)) for w, dy in far_off]
    peers += sum_peers[::-1] + [partner]
    for peer in peers[:14]:
        pl.semaphore_signal(bar, inc=1, device_id=peer, device_id_type=MESH)

    def flatten(src, flat):
        flat[...] = src[...].astype(F32).reshape(TOK * NH, DH)

    def pick(flat, h):
        return flat[pl.ds(h, TOK, stride=NH), :]

    def place(flat, h, value):
        flat[pl.ds(h, TOK, stride=NH), :] = value

    def by_four(body):
        def step(i, _):
            body([4 * i + u for u in range(4)])
            return 0

        lax.fori_loop(0, HALF // 4, step, 0)

    rows = lax.broadcasted_iota(jnp.int32, (TOK, TOK), 0)
    cols = lax.broadcasted_iota(jnp.int32, (TOK, TOK), 1)
    causal = cols <= rows

    def copy(sems, k, src, dst, to):
        return pltpu.make_async_remote_copy(
            src_ref=src, dst_ref=dst, send_sem=sems[0].at[k], recv_sem=sems[1].at[k],
            device_id=to, device_id_type=MESH,
        )

    d2d_sems, pair_sems, far_sems = (d2d_send, d2d_recv), (pair_send, pair_recv), (far_send, far_recv)

    def state_swap(n):
        return copy(d2d_sems, n, given.at[n], state.at[0, c, n], sibling)

    def state_swap_wait(n):
        return copy(d2d_sems, n, given.at[n], state.at[0, oc, n], sibling)

    def lending(i):
        return copy(d2d_sems, CHUNKS + i, lend.at[i], borrow.at[i], sibling)

    def returning(i):
        return copy(d2d_sems, CHUNKS + 4 + i, give_back.at[i], take_back.at[i], sibling)

    def returning_part(i, n):
        part = pl.ds(n * CH, CH)
        return copy(
            d2d_sems, CHUNKS + 4 + 2 * (n + 1) + i - 2, give_back.at[i, part], take_back.at[i, part], sibling
        )

    def pair_up(j, n):
        return copy(pair_sems, (j, 0, n), theirs.at[j, n], got.at[j, n], partner)

    def pair_down(j, n):
        return copy(pair_sems, (j, 1, n), relay.at[j, n], lent.at[j, n], partner)

    def far(j, way, n):
        return copy(
            far_sems, (j, way, n), joint.at[j, n, pl.ds(0, 15)], owned.at[j, n, pl.ds(0, 15)], partner
        )

    FAR = [(w, dy) for w in (3, 2, 1, 0) for dy in (2, 1, 3, 0) if w or dy]

    def slot_z(f):
        return ring(z + sign * f) if f < 4 else ring(mate - sign * (f - 4))

    def slot_of(zo):
        t = ring(sign * (zo - z))
        return jnp.where(t < 4, t, 11 - t)

    def cut(value):
        return value.reshape(SPLIT, NY * ROWS, DH)

    def state_of(j, b, n, i):
        return state[j, b, n, pl.ds(i * SPLIT, SPLIT)].reshape(DH, DH)

    def base_of(n, i):
        return jnp.concatenate([base[n, slot_of(i * SPLIT + u)] for u in range(SPLIT)], axis=0)

    def scan(j, make, fill, use, reverse):
        def send_pair(n):
            if j == 0:
                state_swap_wait(n).wait_recv()
            for f in range(NZ):
                zo = slot_z(f)
                total = (state[j, 0, n, zo] + state[j, 1, n, zo]).reshape(NY, ROWS, DH)
                ref = mine if f < 4 else theirs
                ref[j, n, pl.ds(f % 4 * NY, NY)] = total
            pair_up(j, n).start()

        def send_up(n):
            pair_up(j, n).wait_recv()
            joint[j, n] = mine[j, n] + got[j, n]
            for w, dy in FAR:
                yo = lax.rem(y + dy, NY)
                copy(
                    far_sems, (j, 0, n), joint.at[j, n, w * NY + yo], owned.at[j, n, y * 4 + z // 2],
                    at(yo, ring(z + sign * w)),
                ).start()
            owned[j, n, y * 4 + z // 2] = joint[j, n, y]

        def send_down(n):
            far(j, 0, n).wait_recv()
            run = jnp.zeros((ROWS, DH), F32)
            for t in range(15, -1, -1) if reverse else range(16):
                bases[j, n, t] = run
                run = run + owned[j, n, t]
            for w, dy in FAR:
                yr = lax.rem(y + dy, NY)
                zr = ring(z + w - 2 * w * lax.rem(z + w, 2))
                copy(
                    far_sems, (j, 1, n), bases.at[j, n, yr * 4 + zr // 2], early.at[j, n, w * NY + y],
                    at(yr, zr),
                ).start()
            early[j, n, y] = bases[j, n, y * 4 + z // 2]

        chip_first = 1 - odd if reverse else odd

        def send_mate(n):
            far(j, 1, n).wait_recv()
            before = early[j, n]
            relay[j, n] = before + jnp.where(chip_first == 0, mine[j, n], 0.0)
            pair_down(j, n).start()
            own = before + jnp.where(chip_first == 1, got[j, n], 0.0)
            base[n, pl.ds(0, 4)] = own.reshape(4, NY * ROWS, DH)

        def finish_chunk(n):
            pair_down(j, n).wait_recv()
            base[n, pl.ds(4, 4)] = lent[j, n].reshape(4, NY * ROWS, DH)
            heads = [n * CH + i for i in range(CH)]
            first = [base_of(n, i) for i in range(CH)]
            block = 1 if reverse else 0
            second = [f + state_of(j, block, n, i) for i, f in enumerate(first)]
            first, second = [[x.astype(BF16) for x in xs] for xs in (first, second)]
            use(n, heads, *((second, first) if reverse else (first, second)))

        for n in range(CHUNKS + 2 * (1 - j)):
            if n < CHUNKS:
                make(n)
            if j:
                send_pair(n)
            elif 0 <= n - 1 < CHUNKS:
                send_pair(n - 1)
            if j == 0 and n >= 2:
                send_up(n - 2)
        if j:
            for n in range(CHUNKS):
                send_up(n)
        fill("start")
        for n in range(CHUNKS):
            send_down(n)
            fill("down%d" % n)
        for n in range(CHUNKS):
            send_mate(n)
            fill("mate%d" % n)
        for n in range(CHUNKS):
            finish_chunk(n)

    def scan_end(j):
        for n in range(CHUNKS):
            pair_up(j, n).wait_send()
            pair_down(j, n).wait_send()
            far(j, 0, n).wait_send()
            far(j, 1, n).wait_send()

    loads[0].wait()
    flatten(k_in, flat_a)
    for peer in peers[14:]:
        pl.semaphore_signal(bar, inc=1, device_id=peer, device_id_type=MESH)
    loads[1].wait()
    flatten(v_in, flat_b)

    def make_state(n):
        span = range(n * CH, n * CH + CH)
        away = [(pick(flat_a, oc * HALF + i), pick(flat_b, oc * HALF + i)) for i in span]
        here = [(pick(flat_a, c * HALF + i), pick(flat_b, c * HALF + i)) for i in span]
        states = [mm(kk.astype(BF16), vv.astype(BF16), 0, 0) for kk, vv in away + here]
        for u, i in enumerate(span):
            lend[0, i], lend[1, i] = away[u]
            kk, vv = here[u]
            kh[c * HALF + i] = kk.astype(BF16)
            vh[c * HALF + i] = vv.astype(BF16)
            given[n, pl.ds(u * SPLIT, SPLIT)] = cut(states[u])
            state[0, c, n, pl.ds(u * SPLIT, SPLIT)] = cut(states[CH + u])
        if n == 0:
            pl.semaphore_wait(bar, len(peers))
        state_swap(n).start()

    def share(index, flat, ref):
        def body(heads):
            away = [pick(flat, oc * HALF + i) for i in heads]
            here = [pick(flat, c * HALF + i).astype(BF16) for i in heads]
            for i, x, m in zip(heads, away, here):
                lend[index, i] = x
                ref[c * HALF + i] = m

        by_four(body)
        lending(index).start()

    def receive(index, ref):
        lending(index).wait_recv()

        def body(heads):
            for i in heads:
                ref[oc * HALF + i] = borrow[index, i].astype(BF16)

        by_four(body)

    def local_attention(b):
        def body(heads):
            hs = [b * HALF + i for i in heads]
            ws = [jnp.where(causal, mm(qh[h], kh[h], 1, 1), 0.0).astype(BF16) for h in hs]
            outs = [mm(w, vh[h], 1, 0) for h, w in zip(hs, ws)]
            for h, w, o in zip(hs, ws, outs):
                wts[h] = w
                att[h] = o

        by_four(body)

    def lend_query():
        lending(0).start()
        lending(1).start()
        loads[2].wait()
        flatten(q_in, flat_a)
        share(2, flat_a, qh)

    def lend_grad():
        loads[3].wait()
        flatten(g_in, flat_b)
        share(3, flat_b, gh)

    def borrow_three():
        receive(0, kh)
        receive(1, vh)
        receive(2, qh)

    def borrow_grad():
        receive(3, gh)
        acc[...] = jnp.zeros_like(acc)

    forward_work = [
        lend_query, lend_grad, lambda: local_attention(c), borrow_three, lambda: local_attention(oc),
        borrow_grad,
    ]

    def fill_forward(place_name):
        for task in FORWARD_FILL.get(place_name, ()):
            forward_work[task]()

    def attend(n, heads, *priors):
        for b in range(2):
            hs = [b * HALF + i for i in heads]
            parts = [att[h] + mm(qh[h], pr, 1, 0) for h, pr in zip(hs, priors[b])]
            grads = [gh[h].astype(F32) for h in hs]
            for h, pr, a in zip(hs, priors[b], parts):
                prior[h] = pr
                full[h] = a
            acc[b, 0] += sum(a * a for a in parts)
            acc[b, 1] += sum(a * g for a, g in zip(parts, grads))

    scan(0, make_state, fill_forward, attend, False)

    packed = jnp.zeros((TOK, TOK), F32)
    for b in range(2):
        for i in range(2):
            packed = jnp.where(cols == 2 * b + i, jnp.sum(acc[b, i], axis=1, keepdims=True), packed)
    msg[...] = jnp.transpose(packed)[0:8]
    xs = [
        copy((x_send, x_recv), i, msg, sums.at[i], peer) for i, peer in enumerate(sum_peers)
    ]
    for x in xs:
        x.start()
    for x in xs:
        x.wait_recv()
    total = msg[...]
    for i in range(len(xs)):
        total = total + sums[i]
    back = jnp.zeros((TOK, TOK), F32)
    for b in range(2):
        inv = 1.0 / jnp.sqrt(total[2 * b : 2 * b + 1] / ROW_WIDTH + EPS)
        fac = inv * inv * inv * total[2 * b + 1 : 2 * b + 2] / ROW_WIDTH
        back = jnp.where(rows == 2 * b, inv, jnp.where(rows == 2 * b + 1, fac, back))
    back = jnp.transpose(back)
    inv_col = [back[:, 0:1], back[:, 2:3]]
    fac_col = [back[:, 1:2], back[:, 3:4]]

    def make_grad(n):
        span = range(n * CH, n * CH + CH)
        where = [(b, u, b * HALF + i) for b in range(2) for u, i in enumerate(span)]
        ags = [
            (inv_col[b] * gh[h].astype(F32) - full[h] * fac_col[b]).astype(BF16) for b, _, h in where
        ]
        states = [mm(qh[h], ag, 0, 0) for (_, _, h), ag in zip(where, ags)]
        for (b, u, h), ag, st in zip(where, ags, states):
            agr[h] = ag
            state[1, b, n, pl.ds(u * SPLIT, SPLIT)] = cut(st)

    def query_side(b, start, keep):
        scale = jnp.where(b == 0, inv_col[0], inv_col[1])

        def body(heads):
            hs = [b * HALF + i for i in heads]
            ags = [agr[h] for h in hs]
            ms = [jnp.where(causal, mm(ag, vh[h], 1, 1), 0.0).astype(BF16) for h, ag in zip(hs, ags)]
            qgs = [mm(m, kh[h], 1, 0) + mm(ag, prior[h], 1, 1) for h, m, ag in zip(hs, ms, ags)]
            kgs = [mm(m, qh[h], 0, 0) for h, m in zip(hs, ms)]
            vgs = [mm(wts[h], ag, 0, 0) for h, ag in zip(hs, ags)]
            normed = [full[h] * scale for h in hs]
            for u, i in enumerate(heads):
                keep(i, normed[u], qgs[u])
                kg_acc[hs[u]] = kgs[u]
                vg_acc[hs[u]] = vgs[u]

        body([start + u for u in range(4)])

    def keep_away(i, left, right):
        give_back[0, i] = left
        give_back[1, i] = right

    def keep_here(i, left, right):
        place(flat_a, c * HALF + i, left)
        place(flat_b, c * HALF + i, right)

    def emit(flat, ref):
        ref[...] = flat[...].reshape(TOK, NH, DH).astype(BF16)

    def give_two():
        returning(0).start()
        returning(1).start()

    def write_two():
        returning(0).wait_recv()
        returning(1).wait_recv()

        def body(heads):
            for i in heads:
                place(flat_a, oc * HALF + i, take_back[0, i])
                place(flat_b, oc * HALF + i, take_back[1, i])

        by_four(body)
        emit(flat_a, n_out)
        emit(flat_b, qg_out)

    backward_work = [
        lambda: query_side(oc, 0, keep_away), lambda: query_side(oc, 4, keep_away), give_two,
        lambda: query_side(c, 0, keep_here), lambda: query_side(c, 4, keep_here), write_two,
    ]

    def fill_backward(place_name):
        for task in BACKWARD_FILL.get(place_name, ()):
            backward_work[task]()

    def collect(n):
        for i in range(2):
            returning_part(2 + i, n).wait_recv()
        for i in range(n * CH, n * CH + CH):
            place(flat_a, oc * HALF + i, take_back[2, i])
            place(flat_b, oc * HALF + i, take_back[3, i])

    def finish(n, heads, *laters):
        def grads(b):
            hs = [b * HALF + i for i in heads]
            lts = [jnp.where(b == 0, l0, l1) for l0, l1 in zip(*laters)]
            keys = [kg_acc[h] + mm(vh[h], lt, 1, 1) for h, lt in zip(hs, lts)]
            values = [vg_acc[h] + mm(kh[h], lt, 1, 0) for h, lt in zip(hs, lts)]
            return keys, values

        for i, kg, vg in zip(heads, *grads(oc)):
            give_back[2, i] = kg
            give_back[3, i] = vg
        for i in range(2):
            returning_part(2 + i, n).start()
        for i, kg, vg in zip(heads, *grads(c)):
            keep_here(i, kg, vg)
        if n:
            collect(n - 1)

    scan(1, make_grad, fill_backward, finish, True)
    collect(CHUNKS - 1)
    emit(flat_a, kg_out)
    emit(flat_b, vg_out)

    for n in range(CHUNKS):
        state_swap(n).wait_send()
        for i in range(2):
            returning_part(2 + i, n).wait_send()
    for i in range(4):
        lending(i).wait_send()
    for i in range(2):
        returning(i).wait_send()
    scan_end(0)
    scan_end(1)
    for x in xs:
        x.wait_send()


def deliver(*refs):
    sem = refs[8]
    copies = [pltpu.make_async_copy(refs[i], refs[4 + i], sem.at[i]) for i in range(4)]
    for cp in copies:
        cp.start()
    for cp in copies:
        cp.wait()


def shards(queries, keys, values, out_grad):
    shape = (TOK, NH, DH)
    half = (CHUNKS, NZ, NY * ROWS, DH)
    part = (2, CHUNKS, 16, ROWS, DH)
    per = (2, 2, CHUNKS)
    vm = pltpu.VMEM
    dma = pltpu.SemaphoreType.DMA
    hm = (NH, TOK, DH)
    swap = (4, HALF, TOK, DH)
    d2d = 4 + 4 + 3 * CHUNKS
    results = pl.pallas_call(
        kernel,
        out_shape=[jax.ShapeDtypeStruct(shape, BF16)] * 4,
        in_specs=[pl.BlockSpec(memory_space=pltpu.HBM)] * 4,
        out_specs=[pl.BlockSpec(memory_space=pltpu.VMEM)] * 4,
        scratch_shapes=[vm(shape, BF16)] * 4
        + [vm((TOK * NH, DH), F32)] * 2
        + [vm(hm, BF16)] * 7
        + [vm(hm, F32)] * 4
        + [vm(swap, F32)] * 4
        + [vm(half, F32)] * 2
        + [vm((2, 2) + half, F32)]
        + [vm(part, F32)] * 9
        + [vm((2, 2, TOK, DH), F32), vm((8, TOK), F32), vm((7, 8, TOK), F32)]
        + [dma((4,)), dma((d2d,)), dma((d2d,)), dma(per), dma(per), dma(per), dma(per)]
        + [dma((7,)), dma((7,))],
        compiler_params=pltpu.CompilerParams(
            collective_id=0, has_side_effects=True, vmem_limit_bytes=48 << 20
        ),
    )(*[pltpu.with_memory_space_constraint(x, pltpu.HBM) for x in (queries, keys, values, out_grad)])
    return pl.pallas_call(
        deliver,
        out_shape=[jax.ShapeDtypeStruct(shape, BF16)] * 4,
        in_specs=[pl.BlockSpec(memory_space=pltpu.VMEM)] * 4,
        out_specs=[pl.BlockSpec(memory_space=pl.ANY)] * 4,
        scratch_shapes=[dma((4,))],
        compiler_params=pltpu.CompilerParams(vmem_limit_bytes=8 << 20),
    )(*results)


def solution(mesh):
    spec = P("seq", "head", None)
    return jax.shard_map(
        shards, mesh=mesh, in_specs=(spec,) * 4, out_specs=(spec,) * 4, check_vma=False
    )
```

```python
import jax
import jax.numpy as jnp
from jax import lax
from jax.experimental import pallas as pl
from jax.experimental.pallas import tpu as pltpu
from jax.sharding import PartitionSpec as P

EPS = 1e-06
CHIPS = 32
NY, NZ = 4, 8
TOK = 128
NH = 16
DH = 128
HALF = NH // 2
CHUNKS = 4
CH = HALF // CHUNKS
ROWS = CH * DH // CHIPS
SPLIT = NZ // CH
ROW_WIDTH = 64 * DH
MESH = pl.DeviceIdType.MESH
FORWARD_FILL = {"start": (0, 1), "down1": (2,), "down3": (3, 4, 5)}
BACKWARD_FILL = {"start": (0, 1, 2), "down3": (3, 4), "mate3": (5,)}
F32 = jnp.float32
BF16 = jnp.bfloat16


def mm(left, right, lc, rc):
    return lax.dot_general(
        left, right, (((lc,), (rc,)), ((), ())), preferred_element_type=F32
    )


def kernel(
    q_hbm, k_hbm, v_hbm, g_hbm,
    n_out, qg_out, kg_out, vg_out,
    q_in, k_in, v_in, g_in,
    flat_a, flat_b, qh, kh, vh, gh, wts, agr, prior, att, full, kg_acc, vg_acc,
    lend, borrow, give_back, take_back, given, base, state,
    mine, theirs, got, joint, owned, bases, early, relay, lent,
    acc, msg, sums,
    load_sem, d2d_send, d2d_recv, pair_send, pair_recv, far_send, far_recv, x_send, x_recv,
):
    seq, head = lax.axis_index("seq"), lax.axis_index("head")
    s, c = seq // 2, lax.rem(seq, 2)
    oc = 1 - c

    loads = [
        pltpu.make_async_copy(src, dst, load_sem.at[i])
        for i, (src, dst) in enumerate(
            ((k_hbm, k_in), (v_hbm, v_in), (q_hbm, q_in), (g_hbm, g_in))
        )
    ]
    for ld in loads[:2]:
        ld.start()

    y, z = s // NZ, lax.rem(s, NZ)
    odd = lax.rem(z, 2)
    sign = 2 * odd - 1
    mate = z - sign

    def at(yy, zz):
        return ((yy * NZ + zz) * 2 + c, head)

    def ring(zz):
        return lax.rem(zz + NZ, NZ)

    bar = pltpu.get_barrier_semaphore()
    sibling, partner = (2 * s + oc, head), at(y, mate)
    sum_peers = [sibling] + [
        (2 * s + cc, lax.rem(head + i, 4)) for i in range(1, 4) for cc in (c, oc)
    ]
    far_off = sorted(
        [(w, dy) for w in (0, 1, 2, 3, -2) for dy in range(NY) if w or dy],
        key=lambda o: -(abs(o[0]) + min(o[1], NY - o[1])),
    )
    peers = [at(lax.rem(y + dy, NY), ring(z + sign * w)) for w, dy in far_off]
    peers += sum_peers[::-1] + [partner]
    for peer in peers[:14]:
        pl.semaphore_signal(bar, inc=1, device_id=peer, device_id_type=MESH)

    def flatten(src, flat):
        flat[...] = src[...].astype(F32).reshape(TOK * NH, DH)

    def pick(flat, h):
        return flat[pl.ds(h, TOK, stride=NH), :]

    def place(flat, h, value):
        flat[pl.ds(h, TOK, stride=NH), :] = value

    def by_four(body):
        def step(i, _):
            body([4 * i + u for u in range(4)])
            return 0

        lax.fori_loop(0, HALF // 4, step, 0)

    rows = lax.broadcasted_iota(jnp.int32, (TOK, TOK), 0)
    cols = lax.broadcasted_iota(jnp.int32, (TOK, TOK), 1)
    causal = cols <= rows

    def copy(sems, k, src, dst, to):
        return pltpu.make_async_remote_copy(
            src_ref=src, dst_ref=dst, send_sem=sems[0].at[k], recv_sem=sems[1].at[k],
            device_id=to, device_id_type=MESH,
        )

    d2d_sems, pair_sems, far_sems = (d2d_send, d2d_recv), (pair_send, pair_recv), (far_send, far_recv)

    def state_swap(n):
        return copy(d2d_sems, n, given.at[n], state.at[0, c, n], sibling)

    def state_swap_wait(n):
        return copy(d2d_sems, n, given.at[n], state.at[0, oc, n], sibling)

    def lending(i):
        return copy(d2d_sems, CHUNKS + i, lend.at[i], borrow.at[i], sibling)

    def returning(i):
        return copy(d2d_sems, CHUNKS + 4 + i, give_back.at[i], take_back.at[i], sibling)

    def returning_part(i, n):
        part = pl.ds(n * CH, CH)
        return copy(
            d2d_sems, CHUNKS + 4 + 2 * (n + 1) + i - 2, give_back.at[i, part], take_back.at[i, part], sibling
        )

    def pair_up(j, n):
        return copy(pair_sems, (j, 0, n), theirs.at[j, n], got.at[j, n], partner)

    def pair_down(j, n):
        return copy(pair_sems, (j, 1, n), relay.at[j, n], lent.at[j, n], partner)

    def far(j, way, n):
        return copy(
            far_sems, (j, way, n), joint.at[j, n, pl.ds(0, 15)], owned.at[j, n, pl.ds(0, 15)], partner
        )

    FAR = [(w, dy) for w in (3, 2, 1, 0) for dy in (2, 1, 3, 0) if w or dy]

    def slot_z(f):
        return ring(z + sign * f) if f < 4 else ring(mate - sign * (f - 4))

    def slot_of(zo):
        t = ring(sign * (zo - z))
        return jnp.where(t < 4, t, 11 - t)

    def cut(value):
        return value.reshape(SPLIT, NY * ROWS, DH)

    def state_of(j, b, n, i):
        return state[j, b, n, pl.ds(i * SPLIT, SPLIT)].reshape(DH, DH)

    def base_of(n, i):
        return jnp.concatenate([base[n, slot_of(i * SPLIT + u)] for u in range(SPLIT)], axis=0)

    def scan(j, make, fill, use, reverse):
        def send_pair(n):
            if j == 0:
                state_swap_wait(n).wait_recv()
            for f in range(NZ):
                zo = slot_z(f)
                total = (state[j, 0, n, zo] + state[j, 1, n, zo]).reshape(NY, ROWS, DH)
                ref = mine if f < 4 else theirs
                ref[j, n, pl.ds(f % 4 * NY, NY)] = total
            pair_up(j, n).start()

        def send_up(n):
            pair_up(j, n).wait_recv()
            joint[j, n] = mine[j, n] + got[j, n]
            for w, dy in FAR:
                yo = lax.rem(y + dy, NY)
                copy(
                    far_sems, (j, 0, n), joint.at[j, n, w * NY + yo], owned.at[j, n, y * 4 + z // 2],
                    at(yo, ring(z + sign * w)),
                ).start()
            owned[j, n, y * 4 + z // 2] = joint[j, n, y]

        def send_down(n):
            far(j, 0, n).wait_recv()
            run = jnp.zeros((ROWS, DH), F32)
            for t in range(15, -1, -1) if reverse else range(16):
                bases[j, n, t] = run
                run = run + owned[j, n, t]
            for w, dy in FAR:
                yr = lax.rem(y + dy, NY)
                zr = ring(z + w - 2 * w * lax.rem(z + w, 2))
                copy(
                    far_sems, (j, 1, n), bases.at[j, n, yr * 4 + zr // 2], early.at[j, n, w * NY + y],
                    at(yr, zr),
                ).start()
            early[j, n, y] = bases[j, n, y * 4 + z // 2]

        chip_first = 1 - odd if reverse else odd

        def send_mate(n):
            far(j, 1, n).wait_recv()
            before = early[j, n]
            relay[j, n] = before + jnp.where(chip_first == 0, mine[j, n], 0.0)
            pair_down(j, n).start()
            own = before + jnp.where(chip_first == 1, got[j, n], 0.0)
            base[n, pl.ds(0, 4)] = own.reshape(4, NY * ROWS, DH)

        def finish_chunk(n):
            pair_down(j, n).wait_recv()
            base[n, pl.ds(4, 4)] = lent[j, n].reshape(4, NY * ROWS, DH)
            heads = [n * CH + i for i in range(CH)]
            first = [base_of(n, i) for i in range(CH)]
            block = 1 if reverse else 0
            second = [f + state_of(j, block, n, i) for i, f in enumerate(first)]
            first, second = [[x.astype(BF16) for x in xs] for xs in (first, second)]
            use(n, heads, *((second, first) if reverse else (first, second)))

        for n in range(CHUNKS + 2 * (1 - j)):
            if n < CHUNKS:
                make(n)
            if j:
                send_pair(n)
            elif 0 <= n - 1 < CHUNKS:
                send_pair(n - 1)
            if j == 0 and n >= 2:
                send_up(n - 2)
        if j:
            for n in range(CHUNKS):
                send_up(n)
        fill("start")
        for n in range(CHUNKS):
            send_down(n)
            fill("down%d" % n)
        for n in range(CHUNKS):
            send_mate(n)
            fill("mate%d" % n)
        for n in range(CHUNKS):
            finish_chunk(n)

    def scan_end(j):
        for n in range(CHUNKS):
            pair_up(j, n).wait_send()
            pair_down(j, n).wait_send()
            far(j, 0, n).wait_send()
            far(j, 1, n).wait_send()

    loads[0].wait()
    flatten(k_in, flat_a)
    for peer in peers[14:]:
        pl.semaphore_signal(bar, inc=1, device_id=peer, device_id_type=MESH)
    loads[1].wait()
    for ld in loads[2:]:
        ld.start()
    flatten(v_in, flat_b)

    def make_state(n):
        span = range(n * CH, n * CH + CH)
        away = [(pick(flat_a, oc * HALF + i), pick(flat_b, oc * HALF + i)) for i in span]
        here = [(pick(flat_a, c * HALF + i), pick(flat_b, c * HALF + i)) for i in span]
        states = [mm(kk.astype(BF16), vv.astype(BF16), 0, 0) for kk, vv in away + here]
        for u, i in enumerate(span):
            lend[0, i], lend[1, i] = away[u]
            kk, vv = here[u]
            kh[c * HALF + i] = kk.astype(BF16)
            vh[c * HALF + i] = vv.astype(BF16)
            given[n, pl.ds(u * SPLIT, SPLIT)] = cut(states[u])
            state[0, c, n, pl.ds(u * SPLIT, SPLIT)] = cut(states[CH + u])
        if n == 0:
            pl.semaphore_wait(bar, len(peers))
        state_swap(n).start()

    def share(index, flat, ref):
        def body(heads):
            away = [pick(flat, oc * HALF + i) for i in heads]
            here = [pick(flat, c * HALF + i).astype(BF16) for i in heads]
            for i, x, m in zip(heads, away, here):
                lend[index, i] = x
                ref[c * HALF + i] = m

        by_four(body)
        lending(index).start()

    def receive(index, ref):
        lending(index).wait_recv()

        def body(heads):
            for i in heads:
                ref[oc * HALF + i] = borrow[index, i].astype(BF16)

        by_four(body)

    def local_attention(b):
        def body(heads):
            hs = [b * HALF + i for i in heads]
            ws = [jnp.where(causal, mm(qh[h], kh[h], 1, 1), 0.0).astype(BF16) for h in hs]
            outs = [mm(w, vh[h], 1, 0) for h, w in zip(hs, ws)]
            for h, w, o in zip(hs, ws, outs):
                wts[h] = w
                att[h] = o

        by_four(body)

    def lend_query():
        lending(0).start()
        lending(1).start()
        loads[2].wait()
        flatten(q_in, flat_a)
        share(2, flat_a, qh)

    def lend_grad():
        loads[3].wait()
        flatten(g_in, flat_b)
        share(3, flat_b, gh)

    def borrow_three():
        receive(0, kh)
        receive(1, vh)
        receive(2, qh)

    def borrow_grad():
        receive(3, gh)
        acc[...] = jnp.zeros_like(acc)

    forward_work = [
        lend_query, lend_grad, lambda: local_attention(c), borrow_three, lambda: local_attention(oc),
        borrow_grad,
    ]

    def fill_forward(place_name):
        for task in FORWARD_FILL.get(place_name, ()):
            forward_work[task]()

    def attend(n, heads, *priors):
        for b in range(2):
            hs = [b * HALF + i for i in heads]
            parts = [att[h] + mm(qh[h], pr, 1, 0) for h, pr in zip(hs, priors[b])]
            grads = [gh[h].astype(F32) for h in hs]
            for h, pr, a in zip(hs, priors[b], parts):
                prior[h] = pr
                full[h] = a
            acc[b, 0] += sum(a * a for a in parts)
            acc[b, 1] += sum(a * g for a, g in zip(parts, grads))

    scan(0, make_state, fill_forward, attend, False)

    packed = jnp.zeros((TOK, TOK), F32)
    for b in range(2):
        for i in range(2):
            packed = jnp.where(cols == 2 * b + i, jnp.sum(acc[b, i], axis=1, keepdims=True), packed)
    msg[...] = jnp.transpose(packed)[0:8]
    xs = [
        copy((x_send, x_recv), i, msg, sums.at[i], peer) for i, peer in enumerate(sum_peers)
    ]
    for x in xs:
        x.start()
    for x in xs:
        x.wait_recv()
    total = msg[...]
    for i in range(len(xs)):
        total = total + sums[i]
    back = jnp.zeros((TOK, TOK), F32)
    for b in range(2):
        inv = 1.0 / jnp.sqrt(total[2 * b : 2 * b + 1] / ROW_WIDTH + EPS)
        fac = inv * inv * inv * total[2 * b + 1 : 2 * b + 2] / ROW_WIDTH
        back = jnp.where(rows == 2 * b, inv, jnp.where(rows == 2 * b + 1, fac, back))
    back = jnp.transpose(back)
    inv_col = [back[:, 0:1], back[:, 2:3]]
    fac_col = [back[:, 1:2], back[:, 3:4]]

    def make_grad(n):
        span = range(n * CH, n * CH + CH)
        where = [(b, u, b * HALF + i) for b in range(2) for u, i in enumerate(span)]
        ags = [
            (inv_col[b] * gh[h].astype(F32) - full[h] * fac_col[b]).astype(BF16) for b, _, h in where
        ]
        states = [mm(qh[h], ag, 0, 0) for (_, _, h), ag in zip(where, ags)]
        for (b, u, h), ag, st in zip(where, ags, states):
            agr[h] = ag
            state[1, b, n, pl.ds(u * SPLIT, SPLIT)] = cut(st)

    def query_side(b, start, keep):
        scale = jnp.where(b == 0, inv_col[0], inv_col[1])

        def body(heads):
            hs = [b * HALF + i for i in heads]
            ags = [agr[h] for h in hs]
            ms = [jnp.where(causal, mm(ag, vh[h], 1, 1), 0.0).astype(BF16) for h, ag in zip(hs, ags)]
            qgs = [mm(m, kh[h], 1, 0) + mm(ag, prior[h], 1, 1) for h, m, ag in zip(hs, ms, ags)]
            kgs = [mm(m, qh[h], 0, 0) for h, m in zip(hs, ms)]
            vgs = [mm(wts[h], ag, 0, 0) for h, ag in zip(hs, ags)]
            normed = [full[h] * scale for h in hs]
            for u, i in enumerate(heads):
                keep(i, normed[u], qgs[u])
                kg_acc[hs[u]] = kgs[u]
                vg_acc[hs[u]] = vgs[u]

        body([start + u for u in range(4)])

    def keep_away(i, left, right):
        give_back[0, i] = left
        give_back[1, i] = right

    def keep_here(i, left, right):
        place(flat_a, c * HALF + i, left)
        place(flat_b, c * HALF + i, right)

    def emit(flat, ref):
        ref[...] = flat[...].reshape(TOK, NH, DH).astype(BF16)

    def give_two():
        returning(0).start()
        returning(1).start()

    def write_two():
        returning(0).wait_recv()
        returning(1).wait_recv()

        def body(heads):
            for i in heads:
                place(flat_a, oc * HALF + i, take_back[0, i])
                place(flat_b, oc * HALF + i, take_back[1, i])

        by_four(body)
        emit(flat_a, n_out)
        emit(flat_b, qg_out)

    backward_work = [
        lambda: query_side(oc, 0, keep_away), lambda: query_side(oc, 4, keep_away), give_two,
        lambda: query_side(c, 0, keep_here), lambda: query_side(c, 4, keep_here), write_two,
    ]

    def fill_backward(place_name):
        for task in BACKWARD_FILL.get(place_name, ()):
            backward_work[task]()

    def collect(n):
        for i in range(2):
            returning_part(2 + i, n).wait_recv()
        for i in range(n * CH, n * CH + CH):
            place(flat_a, oc * HALF + i, take_back[2, i])
            place(flat_b, oc * HALF + i, take_back[3, i])

    def finish(n, heads, *laters):
        def grads(b):
            hs = [b * HALF + i for i in heads]
            lts = [jnp.where(b == 0, l0, l1) for l0, l1 in zip(*laters)]
            keys = [kg_acc[h] + mm(vh[h], lt, 1, 1) for h, lt in zip(hs, lts)]
            values = [vg_acc[h] + mm(kh[h], lt, 1, 0) for h, lt in zip(hs, lts)]
            return keys, values

        for i, kg, vg in zip(heads, *grads(oc)):
            give_back[2, i] = kg
            give_back[3, i] = vg
        for i in range(2):
            returning_part(2 + i, n).start()
        for i, kg, vg in zip(heads, *grads(c)):
            keep_here(i, kg, vg)
        if n:
            collect(n - 1)

    scan(1, make_grad, fill_backward, finish, True)
    collect(CHUNKS - 1)
    emit(flat_a, kg_out)
    emit(flat_b, vg_out)

    for n in range(CHUNKS):
        state_swap(n).wait_send()
        for i in range(2):
            returning_part(2 + i, n).wait_send()
    for i in range(4):
        lending(i).wait_send()
    for i in range(2):
        returning(i).wait_send()
    scan_end(0)
    scan_end(1)
    for x in xs:
        x.wait_send()


def deliver(*refs):
    sem = refs[8]
    copies = [pltpu.make_async_copy(refs[i], refs[4 + i], sem.at[i]) for i in range(4)]
    for cp in copies:
        cp.start()
    for cp in copies:
        cp.wait()


def shards(queries, keys, values, out_grad):
    shape = (TOK, NH, DH)
    half = (CHUNKS, NZ, NY * ROWS, DH)
    part = (2, CHUNKS, 16, ROWS, DH)
    per = (2, 2, CHUNKS)
    vm = pltpu.VMEM
    dma = pltpu.SemaphoreType.DMA
    hm = (NH, TOK, DH)
    swap = (4, HALF, TOK, DH)
    d2d = 4 + 4 + 3 * CHUNKS
    results = pl.pallas_call(
        kernel,
        out_shape=[jax.ShapeDtypeStruct(shape, BF16)] * 4,
        in_specs=[pl.BlockSpec(memory_space=pltpu.HBM)] * 4,
        out_specs=[pl.BlockSpec(memory_space=pltpu.VMEM)] * 4,
        scratch_shapes=[vm(shape, BF16)] * 4
        + [vm((TOK * NH, DH), F32)] * 2
        + [vm(hm, BF16)] * 7
        + [vm(hm, F32)] * 4
        + [vm(swap, F32)] * 4
        + [vm(half, F32)] * 2
        + [vm((2, 2) + half, F32)]
        + [vm(part, F32)] * 9
        + [vm((2, 2, TOK, DH), F32), vm((8, TOK), F32), vm((7, 8, TOK), F32)]
        + [dma((4,)), dma((d2d,)), dma((d2d,)), dma(per), dma(per), dma(per), dma(per)]
        + [dma((7,)), dma((7,))],
        compiler_params=pltpu.CompilerParams(
            collective_id=0, has_side_effects=True, vmem_limit_bytes=48 << 20
        ),
    )(*[pltpu.with_memory_space_constraint(x, pltpu.HBM) for x in (queries, keys, values, out_grad)])
    return pl.pallas_call(
        deliver,
        out_shape=[jax.ShapeDtypeStruct(shape, BF16)] * 4,
        in_specs=[pl.BlockSpec(memory_space=pltpu.VMEM)] * 4,
        out_specs=[pl.BlockSpec(memory_space=pl.ANY)] * 4,
        scratch_shapes=[dma((4,))],
        compiler_params=pltpu.CompilerParams(vmem_limit_bytes=8 << 20),
    )(*results)


def solution(mesh):
    spec = P("seq", "head", None)
    return jax.shard_map(
        shards, mesh=mesh, in_specs=(spec,) * 4, out_specs=(spec,) * 4, check_vma=False
    )
```
